32 devices in a mesh: lon: 8 (over z, y), lat: 4 (over x, core).
Axes of the slice: x: 2, y: 2, z: 4, core: 2. Of those that a mesh axis runs over, the one named last changes fastest.
Arguments:
- tracers: float32 [2, 4, 64, 1024], P(None, None, 'lat', 'lon'), may hold values from -6 to 6
- land_mask: int32 [64, 1024], P('lat', 'lon'), may hold values 0 or 1
- level_counts: int32 [64, 1024], P('lat', 'lon'), may hold values from 1 to 4
- fold_partner: int32 [1024], P('lon'), may hold values from 0 to 1023, as said below
- cotangent: float32 [2, 4, 64, 1024], P(None, None, 'lat', 'lon'), may hold values from -6 to 6
- w_first: float32 [6, 128], replicated, may hold values from -2.5 to 2.5
- b_first: float32 [128], replicated, may hold values from -3 to 3
- w_second: float32 [128, 128], replicated, may hold values from -0.5 to 0.5
- b_second: float32 [128], replicated, may hold values from -3 to 3
- w_head: float32 [128], replicated, may hold values from -0.5 to 0.5
- b_head: float32 [1], replicated, may hold values from -3 to 3
Outputs:
- tracers_out: float32 [2, 4, 64, 1024], P(None, None, 'lat', 'lon')
- tracer_grad: float32 [2, 4, 64, 1024], P(None, None, 'lat', 'lon')
- w_first_grad: float32 [6, 128], replicated
- w_second_grad: float32 [128, 128], replicated
- w_head_grad: float32 [128], replicated
The draws below stay inside these ranges and needn't reach their ends.
Inputs may be any that keep to these rules, and one draw needn't show every extreme that they name: fold_partner[x] = (s - x) mod 1024 for one odd whole number s of the draw: the mirror about the fold line, so fold_partner[fold_partner[x]] = x and fold_partner[x] != x.
All inputs are finite; a program needn't handle non-finite values. No bound on the sum of `land_mask` on one device may be relied on, other than what follows from the above.
Results may differ from the reference program's by a relative error of at most 0.0003.
Values sent between devices are 32-bit elements; how exact they have to be, the bound alone decides.
No kernel may reach another device: no remote copies, remote signals or barrier semaphores. Data moves between devices by JAX's collectives and lax.ppermute only.
A program may use at most 128 MiB of HBM per device.

```python
import math
import jax
import jax.numpy as jnp
from jax import lax

NZ = 4
HID = 128
FEAT = 6
STEPS = 2
NX = 1024
NY = 64


def draw_fold_partner(key, part):
    key = jax.random.fold_in(key, 7)
    offset = 2 * jax.random.randint(key, (), 0, NX // 2).astype(jnp.int32) + 1
    columns = jnp.arange(NX, dtype=jnp.int32)
    return jnp.mod(offset - columns, NX).astype(jnp.int32)


def with_ends(drawn, stream_key, low, top_value):
    extent = drawn.shape
    place = [jax.random.randint(jax.random.fold_in(stream_key, axis), (), 0, extent[axis]) for axis in range(len(extent))]
    drawn = drawn.at[tuple(place)].set(low)
    longest = extent.index(max(extent))
    place[longest] = (place[longest] + 1) % extent[longest]
    return drawn.at[tuple(place)].set(top_value)


def steps_of(stream_key, extent, split, smallest, high):
    level = 1.0
    for dim, parts in split:
        steps = jax.random.uniform(jax.random.fold_in(jax.random.fold_in(stream_key, 6), dim), (parts,), jnp.float32, smallest / len(split), high / len(split))
        level = level * jnp.repeat(jnp.exp(steps), extent[dim] // parts).reshape((-1,) + (1,) * (len(extent) - 1 - dim))
    return level


def noise(key, extent, width, most, cuts=(), kind=jnp.bfloat16):
    level = steps_of(key, extent, cuts, -0.22, 0.18) if cuts else 1.0
    values = jax.random.normal(key, extent, jnp.float32) * width * level
    return jnp.minimum(jnp.maximum(values, -most), most).astype(kind)


def setup_inputs(seed: int = 0) -> dict:
    seeds = jax.random.split(jax.random.key(seed), 12)
    tracers = noise(seeds[0], (2, NZ, NY, NX), 1.0, 6.0, ((2, 4), (3, 8)), jnp.float32)
    land_mask = with_ends((jax.random.randint(seeds[1], (NY, NX), 0, 5) < 4).astype(jnp.int32), jax.random.fold_in(seeds[1], 1), 0, 1)
    level_counts = with_ends(jax.random.randint(seeds[2], (NY, NX), 1, NZ + 1), jax.random.fold_in(seeds[2], 1), 1, NZ).astype(jnp.int32)
    fold_partner = draw_fold_partner(jax.random.fold_in(seeds[11], 71), 0)
    cotangent = noise(seeds[4], (2, NZ, NY, NX), 1.0, 6.0, ((2, 4), (3, 8)), jnp.float32)
    w_first = noise(seeds[5], (FEAT, HID), FEAT ** -0.5, 2.5, (), jnp.float32)
    b_first = noise(seeds[6], (HID,), 0.5, 3.0, (), jnp.float32)
    w_second = noise(seeds[7], (HID, HID), HID ** -0.5, 0.5, (), jnp.float32)
    b_second = noise(seeds[8], (HID,), 0.5, 3.0, (), jnp.float32)
    w_head = noise(seeds[9], (HID,), HID ** -0.5, 0.5, (), jnp.float32)
    b_head = noise(seeds[10], (1,), 1.0, 3.0, (), jnp.float32)
    return {"tracers": tracers, "land_mask": land_mask, "level_counts": level_counts, "fold_partner": fold_partner, "cotangent": cotangent, "w_first": w_first, "b_first": b_first, "w_second": w_second, "b_second": b_second, "w_head": w_head, "b_head": b_head}


KMAX = 0.24
HIGH = lax.Precision.HIGHEST

def features(tracer, wet_cells):
    rest = [(0, 0)] * (tracer.ndim - 2)
    vertical = (tracer[:, 1:] - tracer[:, :-1]) * (wet_cells[1:] * wet_cells[:-1])
    upward = jnp.pad(-vertical, [(0, 0), (1, 0)] + rest)
    downward = jnp.pad(vertical, [(0, 0), (0, 1)] + rest)
    return jnp.concatenate([tracer, upward, downward], 0)

def closure(flat, w_first, b_first, w_second, b_second, w_head, b_head):
    first = jnp.tanh(jnp.dot(w_first.T, flat, precision=HIGH) + b_first[:, None])
    second = jnp.tanh(jnp.dot(w_second.T, first, precision=HIGH) + b_second[:, None])
    return jnp.dot(w_head, second, precision=HIGH) + b_head[0]

def global_kappa(tracer, wet_cells, weights):
    feats = features(tracer, wet_cells)
    levels_first = jnp.moveaxis(feats, 1, 0).reshape(NZ, FEAT, NY * NX)
    runner = jax.checkpoint(lambda block: closure(block, *weights))
    output = lax.map(runner, levels_first).reshape(NZ, NY, NX)
    return KMAX * jax.nn.sigmoid(output) * wet_cells

def shifted(field, partner):
    east = jnp.roll(field, -1, -1)
    west = jnp.roll(field, 1, -1)
    top_row = jnp.take(field[..., -1:, :], partner, axis=-1)
    north = jnp.concatenate([field[..., 1:, :], top_row], -2)
    south = jnp.concatenate([jnp.zeros_like(field[..., :1, :]), field[..., :-1, :]], -2)
    return [east, west, north, south]

def advance(tracer, wet_cells, partner, weights):
    kappa = global_kappa(tracer, wet_cells, weights)
    change = jnp.zeros_like(tracer)
    for t_side, k_side, w_side in zip(shifted(tracer, partner), shifted(kappa, partner), shifted(wet_cells, partner)):
        coefficient = 0.5 * (kappa + k_side) * wet_cells * w_side
        change = change + coefficient * (t_side - tracer)
    return tracer + change

def reference(tracers, land_mask, level_counts, fold_partner, cotangent, w_first, b_first, w_second, b_second, w_head, b_head):
    below = (jnp.arange(NZ, dtype=jnp.int32)[:, None, None] < level_counts[None]).astype(jnp.float32)
    wet_cells = land_mask[None].astype(jnp.float32) * below

    def forward(start, first, second, head_row):
        weights = (first, b_first, second, b_second, head_row, b_head)
        current = start
        for number in range(STEPS):
            current = advance(current, wet_cells, fold_partner, weights)
        return current
    final, pullback = jax.vjp(forward, tracers, w_first, w_second, w_head)
    grads = pullback(cotangent)
    scale = 1.0 / math.sqrt(NX * NY * NZ)
    return (final, grads[0], grads[1] * scale, grads[2] * scale, grads[3] * scale)
```

```python
import functools
import math

import jax
import jax.numpy as jnp
from jax import lax
from jax.experimental import pallas as pl
from jax.experimental.pallas import tpu as pltpu
from jax.sharding import PartitionSpec as P

KMAX = 0.24
DEPTH = 4
HID = 128
LANES = 128
HALO = 3
SLOT = 2 * HALO
F32 = jnp.float32
BF16 = jnp.bfloat16


def split(x):
    high = x.astype(BF16)
    low = (x - high.astype(F32)).astype(BF16)
    return high, low


def iota(shape, dim):
    return lax.broadcasted_iota(jnp.int32, shape, dim)


def pack_rows_kernel(rows, tracer, cot, land, levels, south, north):
    depth = (land[...] * levels[...]).astype(F32)
    for out, first in ((south, 0), (north, rows - HALO)):
        for j in range(HALO):
            out[8 * j : 8 * j + 8, :] = tracer[pl.ds(first + j, 8, stride=rows), :]
        skip = 0 if first == 0 else 1
        for j in range(2):
            out[24 + 8 * j : 32 + 8 * j, :] = cot[pl.ds(first + skip + j, 8, stride=rows), :]
        out[40:48, :] = jnp.concatenate(
            [depth[first : first + HALO], jnp.zeros((8 - HALO, LANES), F32)], 0
        )


def weights_kernel(w1, b1, w2, b2, wh, a1_out, w2t_out, w2_out, t1_out, col_out):
    first = w1[...]
    bias_high, bias_low = split(b1[...])
    row = iota((16, LANES), 0)
    pad_row = iota((16, LANES), 0)
    for k in range(DEPTH):
        block = jnp.zeros((16, LANES), F32)
        for t in range(2):
            block = jnp.where(row == t * 4 + k, first[t : t + 1], block)
            if k >= 1:
                block = jnp.where(row == 8 + t * 4 + k - 1, -first[2 + t : 3 + t], block)
            block = jnp.where(row == 8 + t * 4 + k, first[4 + t : 5 + t], block)
        high, low = split(block)
        high32, low32 = high.astype(F32), low.astype(F32)
        tail = jnp.where(
            pad_row == 0,
            bias_high.astype(F32),
            jnp.where(pad_row == 1, bias_low.astype(F32), 0.0),
        )
        tall = jnp.concatenate([high32, high32, low32, tail, jnp.zeros((64, LANES), F32)], 0)
        a1_out[k * HID : (k + 1) * HID, :] = jnp.transpose(tall)[:, :64].astype(BF16)
        t1_out[k * 32 : k * 32 + 16, :] = jnp.concatenate([high, high], 1)
        t1_out[k * 32 + 16 : k * 32 + 32, :] = jnp.concatenate([low, jnp.zeros_like(low)], 1)
    second = w2[...]
    for out, matrix in ((w2_out, second), (w2t_out, jnp.transpose(second))):
        high, low = split(matrix)
        out[0:HID, :] = jnp.concatenate([high, high], 1)
        out[HID : 2 * HID, :] = jnp.concatenate([low, low], 1)
    for place, vector in ((0, b2), (HID, wh)):
        column = jnp.transpose(jnp.broadcast_to(vector[...], (HID, LANES)))
        col_out[place : place + HID, :] = jnp.concatenate([column, column], 1)


def assemble_kernel(
    rows, partner, from_north, from_south, fold_near, fold_far, tracer, cot, land, levels, ext, packed
):
    lane = iota((8, LANES), 1)
    at_top = lax.axis_index("lat") == lax.axis_size("lat") - 1
    offset = jnp.bitwise_and(partner[0], LANES - 1)
    source = jnp.bitwise_and(offset - lane, LANES - 1)

    def mirrored(place):
        both = jnp.where(
            lane <= offset, fold_near[place : place + 8, :], fold_far[place : place + 8, :]
        )
        return jnp.take_along_axis(both, source, axis=1)

    def north(plain, folded):
        return jnp.where(at_top, mirrored(folded), from_north[plain : plain + 8, :])

    zero = jnp.zeros((8, LANES), F32)

    def spread(tile, j):
        return jnp.broadcast_to(tile[j : j + 1], (8, LANES))

    depth_here = (land[...] * levels[...]).astype(F32)
    depth_south = from_south[40:48, :]
    depth_north = from_north[40:48, :]
    depth_fold = mirrored(40)
    total = rows + 2 * HALO
    tiles = []
    for i in range(total):
        r = i - HALO
        if r < 0:
            tile_c = from_south[8 * i : 8 * i + 8, :]
            tile_l = from_south[24 + 8 * (i - 1) : 32 + 8 * (i - 1), :] if i >= 1 else zero
            tile_n = spread(depth_south, i)
        elif r < rows:
            tile_c = tracer[pl.ds(r, 8, stride=rows), :]
            tile_l = cot[pl.ds(r, 8, stride=rows), :]
            tile_n = spread(depth_here, r)
        else:
            j = r - rows
            tile_c = north(8 * j, 8 * (2 - j))
            tile_l = north(24 + 8 * j, 24 + 8 * (1 - j)) if j < 2 else zero
            tile_n = jnp.where(at_top, spread(depth_fold, 2 - j), spread(depth_north, j))
        tiles.append((tile_c, tile_l, tile_n))
        for part, tile in enumerate(tiles[-1]):
            ext[24 * i + 8 * part : 24 * i + 8 * part + 8, :] = tile
    for part in range(3):
        acc = zero
        for slot in range(rows + 4):
            moved = pltpu.roll(tiles[slot + 1][part], SLOT * slot + HALO, 1)
            inside = (lane >= SLOT * slot) & (lane < SLOT * slot + SLOT)
            acc = jnp.where(inside, moved, acc)
        packed[8 * part : 8 * part + 8, :] = acc


def steps_kernel(
    rows,
    head_bias,
    ext,
    west_in,
    east_in,
    a1,
    w2t,
    w2,
    t1,
    cols,
    out_tracer,
    out_grad,
    out_sums,
    c_tiles0,
    c_tiles1,
    wv_tiles,
    wet_tiles,
    kappa_tiles,
    slope0,
    slope1,
    d3_tiles,
    bar_tiles,
    x0,
    x1,
    h1b0,
    h1b1,
    h1f0,
    h1f1,
    h2f0,
    h2f1,
    acc_w2,
    acc_a1,
    acc_head,
):
    total = rows + 2 * HALO
    lane = iota((8, LANES), 1)
    level = jnp.bitwise_and(iota((8, LANES), 0), DEPTH - 1)
    level_wide = jnp.bitwise_and(iota((8, 2 * LANES), 0), DEPTH - 1)
    zero = jnp.zeros((8, LANES), F32)
    side_tile = rows
    tile_of = {i: i - HALO for i in range(HALO, rows + HALO)}
    place = rows + 1
    for ring in (1, 2, 3):
        tile_of[HALO - ring] = place
        tile_of[rows + HALO - 1 + ring] = place + 1
        place += 2
    n_tiles = place + (place % 2)
    slots = range(1, rows + 5)

    def east(main, side):
        return (
            pltpu.roll(jnp.where(lane == 0, side, main), LANES - 1, 1),
            pltpu.roll(jnp.where(lane == 0, main, side), LANES - 1, 1),
        )

    def from_west(main, side):
        return (
            pltpu.roll(jnp.where(lane == LANES - 1, side, main), 1, 1),
            pltpu.roll(jnp.where(lane == LANES - 1, main, side), 1, 1),
        )

    def from_west_main(main, side):
        return pltpu.roll(jnp.where(lane == LANES - 1, side, main), 1, 1)

    def unpack(tile, i):
        return pltpu.roll(tile, LANES - (SLOT * (i - 1) + HALO), 1)

    def pack(tiles):
        acc = zero
        for i, tile in tiles.items():
            slot = i - 1
            moved = pltpu.roll(tile, SLOT * slot + HALO, 1)
            inside = (lane >= SLOT * slot) & (lane < SLOT * slot + SLOT)
            acc = jnp.where(inside, moved, acc)
        return acc

    def both(x):
        return x + pltpu.roll(x, 4, 0)

    third = lax.rem(lane, SLOT)
    from_left = third < HALO
    side_c_packed = jnp.where(from_left, west_in[0:8, :], east_in[0:8, :])
    side_l_packed = jnp.where(from_left, west_in[8:16, :], east_in[8:16, :])
    side_n_packed = jnp.where(from_left, west_in[16:24, :], east_in[16:24, :])
    side_lanes = (lane < HALO) | (lane >= LANES - HALO)

    def wet_of(depth):
        return jnp.where(depth > level.astype(F32), 1.0, 0.0)

    def vertical_of(depth):
        inside = (depth > (level + 1).astype(F32)) & (level < DEPTH - 1)
        return jnp.where(inside, 1.0, 0.0)

    c0, wet = {}, {}
    for i in range(total):
        depth = ext[24 * i + 16 : 24 * i + 24, :]
        main_c = ext[24 * i : 24 * i + 8, :]
        main_w = wet_of(depth)
        if i in slots:
            side_c = unpack(side_c_packed, i)
            side_w = jnp.where(side_lanes, wet_of(unpack(side_n_packed, i)), 0.0)
        else:
            side_c, side_w = zero, zero
        c0[i] = (main_c, side_c)
        wet[i] = (main_w, side_w)
        c_tiles0[tile_of[i]] = main_c
        wet_tiles[tile_of[i]] = main_w
        wv_tiles[tile_of[i]] = vertical_of(depth)
    c_tiles0[side_tile] = side_c_packed
    wet_tiles[side_tile] = wet_of(side_n_packed)
    wv_tiles[side_tile] = vertical_of(side_n_packed)
    for tile in range(place, n_tiles):
        c_tiles0[tile] = zero
        wet_tiles[tile] = zero
        wv_tiles[tile] = zero

    def closure(pairs, c_tiles, slope, xs, h1b, h1f, h2f):
        def body(p, carry):
            pieces = []
            for a in range(2):
                c = c_tiles[2 * p + a]
                v = (pltpu.roll(c, 7, 0) - c) * wv_tiles[2 * p + a]
                pieces.append(jnp.concatenate([c, v], 0))
            high, low = split(jnp.concatenate(pieces, 1))
            x = jnp.concatenate([high, low, high, jnp.ones((16, 2 * LANES), BF16)], 0)
            xs[p] = x
            out = jnp.zeros((8, 2 * LANES), F32)
            for k in range(DEPTH):
                h1 = jnp.tanh(
                    jnp.dot(a1[k * HID : (k + 1) * HID, :], x, preferred_element_type=F32)
                )
                h1f[p, k] = h1
                pair = jnp.concatenate(split(h1), 0)
                h1b[p, k] = pair
                z = jnp.dot(w2t[...], pair, preferred_element_type=F32)
                h2 = jnp.tanh(z[:HID] + z[HID:] + cols[0:HID, :])
                h2f[p, k] = h2
                head = jnp.sum(h2 * cols[HID : 2 * HID, :], 0, keepdims=True)
                out = jnp.where(level_wide == k, head, out)
            sig = jax.nn.sigmoid(out + head_bias[0])
            for a in range(2):
                part = sig[:, a * LANES : (a + 1) * LANES]
                kappa = KMAX * part * wet_tiles[2 * p + a]
                kappa_tiles[2 * p + a] = kappa
                slope[2 * p + a] = kappa * (1.0 - part)
            return carry

        lax.fori_loop(0, pairs, body, 0)

    def edge_masks(i):
        east_w = east(*wet[i])
        return tuple(0.5 * a * b for a, b in zip(wet[i], east_w))

    def north_mask(i):
        return tuple(0.5 * a * b for a, b in zip(wet[i], wet[i + 1]))

    def kappas(lo, hi):
        packed = kappa_tiles[side_tile]
        out = {}
        for i in range(lo, hi + 1):
            side = unpack(packed, i) if i in slots else zero
            out[i] = (kappa_tiles[tile_of[i]], side)
        return out

    def coefficients(kappa, lo, hi):
        ce, cn = {}, {}
        for i in range(lo, hi + 1):
            ke = east(*kappa[i])
            ce[i] = tuple(m * (a + b) for m, a, b in zip(edge_masks(i), kappa[i], ke))
        for i in range(lo - 1, hi + 1):
            cn[i] = tuple(
                m * (a + b) for m, a, b in zip(north_mask(i), kappa[i], kappa[i + 1])
            )
        return ce, cn

    def diffs(field, lo, hi):
        de, dn = {}, {}
        for i in range(lo, hi + 1):
            fe = east(*field[i])
            de[i] = tuple(b - a for a, b in zip(field[i], fe))
        for i in range(lo - 1, hi + 1):
            dn[i] = tuple(b - a for a, b in zip(field[i], field[i + 1]))
        return de, dn

    def diffuse(field, ce, cn, de, dn, lo, hi):
        out = {}
        flux_n = {i: tuple(c * d for c, d in zip(cn[i], dn[i])) for i in range(lo - 1, hi + 1)}
        for i in range(lo, hi + 1):
            fe = tuple(c * d for c, d in zip(ce[i], de[i]))
            fw = from_west(*fe)
            out[i] = tuple(
                f + ((a - b) + (c - d))
                for f, a, b, c, d in zip(field[i], fe, fw, flux_n[i], flux_n[i - 1])
            )
        return out

    def kappa_bars(de, dn, le, ln, lo, hi):
        out = {}
        gn = {}
        for i in range(lo - 1, hi + 1):
            gn[i] = tuple(-m * a * b for m, a, b in zip(north_mask(i), dn[i], ln[i]))
        for i in range(lo, hi + 1):
            ge = tuple(-m * a * b for m, a, b in zip(edge_masks(i), de[i], le[i]))
            gw = from_west(*ge)
            out[i] = tuple(
                both((a + b) + (c + d)) for a, b, c, d in zip(ge, gw, gn[i], gn[i - 1])
            )
        return out

    def closure_back(start, pairs, with_sums, slope, xs, h1b, h1f, h2f):
        def body(step, carry):
            p = start + step
            d3 = jnp.concatenate(
                [d3_tiles[2 * p + a] * slope[2 * p + a] for a in range(2)], 1
            )
            bar = jnp.zeros((32, 2 * LANES), F32)
            sum_w2 = None
            sum_head = None
            for k in range(DEPTH):
                h2 = h2f[p, k]
                row = d3[k : k + 1]
                d2 = (cols[HID : 2 * HID, :] * row) * (1.0 - h2 * h2)
                d2b = jnp.concatenate(split(d2), 0)
                e = jnp.dot(w2[...], d2b, preferred_element_type=F32)
                h1 = h1f[p, k]
                d1 = (e[:HID] + e[HID:]) * (1.0 - h1 * h1)
                d1b = jnp.concatenate(split(d1), 0)
                bar = bar + jnp.dot(
                    t1[k * 32 : (k + 1) * 32, :], d1b, preferred_element_type=F32
                )
                if with_sums:
                    part = h2 * row
                    sum_head = part if sum_head is None else sum_head + part
                    outer = lax.dot_general(
                        h1b[p, k], d2b, (((1,), (1,)), ((), ())), preferred_element_type=F32
                    )
                    sum_w2 = outer if sum_w2 is None else sum_w2 + outer
                    acc_a1[k] += lax.dot_general(
                        d1b, xs[p, 0:32, :], (((1,), (1,)), ((), ())), preferred_element_type=F32
                    )
            if with_sums:
                acc_w2[...] += sum_w2
                acc_head[...] += sum_head
            for a in range(2):
                part = bar[:, a * LANES : (a + 1) * LANES]
                part = part[:16] + part[16:]
                v = part[8:] * wv_tiles[2 * p + a]
                bar_tiles[2 * p + a] = part[:8] - v + pltpu.roll(v, 1, 0)
            return carry

        lax.fori_loop(0, pairs, body, 0)

    low, high = HALO, rows + HALO - 1
    closure(n_tiles // 2, c_tiles0, slope0, x0, h1b0, h1f0, h2f0)
    kappa0 = kappas(0, total - 1)
    ce0, cn0 = coefficients(kappa0, low - 2, high + 2)
    de0, dn0 = diffs(c0, low - 2, high + 2)
    c1 = diffuse(c0, ce0, cn0, de0, dn0, low - 2, high + 2)
    for i in range(low - 2, high + 3):
        c_tiles1[tile_of[i]] = c1[i][0]
    c_tiles1[side_tile] = pack({i: c1[i][1] for i in range(low - 2, high + 3)})
    tiles1 = rows + 5
    for tile in range(tiles1, n_tiles):
        c_tiles1[tile] = zero
    closure((tiles1 + 1) // 2, c_tiles1, slope1, x1, h1b1, h1f1, h2f1)
    kappa1 = kappas(low - 2, high + 2)
    ce1, cn1 = coefficients(kappa1, low - 1, high + 1)
    de1, dn1 = diffs(c1, low - 1, high + 1)
    c2 = diffuse(c1, ce1, cn1, de1, dn1, low, high)
    for i in range(low, high + 1):
        out_tracer[pl.ds(i - low, 8, stride=rows), :] = c2[i][0]
    lam2 = {}
    for i in range(low - 2, high + 3):
        lam2[i] = (ext[24 * i + 8 : 24 * i + 16, :], unpack(side_l_packed, i))
    le, ln = diffs(lam2, low - 1, high + 1)
    direct = diffuse(lam2, ce1, cn1, le, ln, low - 1, high + 1)
    bars = kappa_bars(de1, dn1, le, ln, low - 1, high + 1)
    for i in range(low - 1, high + 2):
        d3_tiles[tile_of[i]] = bars[i][0]
    d3_tiles[side_tile] = pack({i: bars[i][1] for i in range(low, high + 1)})
    d3_tiles[rows + 3] = zero
    acc_w2[...] = jnp.zeros_like(acc_w2)
    acc_a1[...] = jnp.zeros_like(acc_a1)
    acc_head[...] = jnp.zeros_like(acc_head)
    closure_back(0, rows // 2, True, slope1, x1, h1b1, h1f1, h2f1)
    closure_back(rows // 2, 2, False, slope1, x1, h1b1, h1f1, h2f1)
    side_bar = bar_tiles[side_tile]
    lam1 = {}
    for i in range(low - 1, high + 2):
        main = direct[i][0] + bar_tiles[tile_of[i]]
        side = direct[i][1] + unpack(side_bar, i)
        lam1[i] = (main, side)
    le, ln = diffs(lam1, low, high)
    direct = diffuse(lam1, ce0, cn0, le, ln, low, high)
    bars = kappa_bars(de0, dn0, le, ln, low, high)
    for i in range(low, high + 1):
        d3_tiles[tile_of[i]] = bars[i][0]
    closure_back(0, rows // 2, True, slope0, x0, h1b0, h1f0, h2f0)
    for i in range(low, high + 1):
        out_grad[pl.ds(i - low, 8, stride=rows), :] = direct[i][0] + bar_tiles[tile_of[i]]
    out_sums[0:HID, :] = (acc_w2[:HID, :HID] + acc_w2[HID:, HID:]) + (
        acc_w2[:HID, HID:] + acc_w2[HID:, :HID]
    )
    first = [None] * 6

    def add(f, value):
        first[f] = value if first[f] is None else first[f] + value

    for k in range(DEPTH):
        cells = acc_a1[k]
        cells = cells[:HID] + cells[HID:]
        cells = jnp.concatenate([cells, jnp.zeros((HID, LANES - 32), F32)], 1)
        turned = jnp.transpose(cells)
        turned = turned[0:16] + turned[16:32]
        for t in range(2):
            add(t, turned[t * 4 + k : t * 4 + k + 1])
            if k >= 1:
                add(2 + t, -turned[8 + t * 4 + k - 1 : 8 + t * 4 + k])
            add(4 + t, turned[8 + t * 4 + k : 8 + t * 4 + k + 1])
    head = jnp.sum(jnp.transpose(acc_head[:, :LANES] + acc_head[:, LANES:]), 0, keepdims=True)
    out_sums[HID : HID + 8, :] = jnp.concatenate(first + [head, jnp.zeros_like(head)], 0)


def finish_kernel(scale, mine, other, w1_out, w2_out, wh_out):
    w2_out[...] = (mine[0:HID, :] + other[0:HID, :]) * scale
    rest = (mine[HID : HID + 8, :] + other[HID : HID + 8, :]) * scale
    w1_out[...] = rest[0:6]
    wh_out[...] = rest[6:7]


VMEM = pl.BlockSpec(memory_space=pltpu.VMEM)
SMEM = pl.BlockSpec(memory_space=pltpu.SMEM)


def call(kernel, outs, ins, scratch=(), limit=None, flops=1_000_000, size=1_000_000):
    return pl.pallas_call(
        kernel,
        out_shape=outs,
        in_specs=ins,
        out_specs=[VMEM] * len(outs),
        scratch_shapes=list(scratch),
        compiler_params=pltpu.CompilerParams(vmem_limit_bytes=limit),
        cost_estimate=pl.CostEstimate(flops=flops, bytes_accessed=size, transcendentals=0),
    )


def shape(*dims, dtype=F32):
    return jax.ShapeDtypeStruct(dims, dtype)


def per_device(
    tracers,
    land_mask,
    level_counts,
    fold_partner,
    cotangent,
    w_first,
    b_first,
    w_second,
    b_second,
    w_head,
    b_head,
):
    rows, cols = land_mask.shape
    n_lon, n_lat = lax.axis_size("lon"), lax.axis_size("lat")
    tracer2 = tracers.reshape(8 * rows, cols)
    cot2 = cotangent.reshape(8 * rows, cols)

    south, north = call(
        functools.partial(pack_rows_kernel, rows), [shape(48, LANES)] * 2, [VMEM] * 4
    )(tracer2, cot2, land_mask, level_counts)
    from_north = lax.ppermute(south, "lat", [(i + 1, i) for i in range(n_lat - 1)])
    from_south = lax.ppermute(north, "lat", [(i, i + 1) for i in range(n_lat - 1)])

    turn = lax.rem(fold_partner[0] // cols + lax.axis_index("lon"), n_lon)

    def across(j, rows_out):
        def pairs(add):
            return [
                (b * n_lat + n_lat - 1, ((j + add - b) % n_lon) * n_lat + n_lat - 1)
                for b in range(n_lon)
            ]

        return (
            lax.ppermute(rows_out, ("lon", "lat"), pairs(0)),
            lax.ppermute(rows_out, ("lon", "lat"), pairs(-1)),
        )

    fold_near, fold_far = lax.switch(
        turn, [functools.partial(across, j) for j in range(n_lon)], north
    )

    a1, w2t, w2, t1, cols_w = call(
        weights_kernel,
        [
            shape(DEPTH * HID, 64, dtype=BF16),
            shape(2 * HID, 2 * HID, dtype=BF16),
            shape(2 * HID, 2 * HID, dtype=BF16),
            shape(DEPTH * 32, 2 * HID, dtype=BF16),
            shape(2 * HID, 2 * LANES),
        ],
        [VMEM] * 5,
    )(w_first, b_first.reshape(1, HID), w_second, b_second.reshape(1, HID), w_head.reshape(1, HID))

    total = rows + 2 * HALO
    ext, packed = call(
        functools.partial(assemble_kernel, rows),
        [shape(24 * total, LANES), shape(24, LANES)],
        [SMEM] + [VMEM] * 8,
    )(
        fold_partner,
        from_north,
        from_south,
        fold_near,
        fold_far,
        tracer2,
        cot2,
        land_mask,
        level_counts,
    )
    from_west = lax.ppermute(packed, "lon", [(i, (i + 1) % n_lon) for i in range(n_lon)])
    from_east = lax.ppermute(packed, "lon", [((i + 1) % n_lon, i) for i in range(n_lon)])

    n_tiles = total + 1 + (total + 1) % 2
    pairs0 = n_tiles // 2
    pairs1 = (rows + 6) // 2
    tiles = pltpu.VMEM((n_tiles, 8, LANES), F32)
    wide = 2 * LANES
    scratch = (
        [tiles] * 9
        + [pltpu.VMEM((n, 64, wide), BF16) for n in (pairs0, pairs1)]
        + [pltpu.VMEM((n, DEPTH, 2 * HID, wide), BF16) for n in (pairs0, pairs1)]
        + [pltpu.VMEM((n, DEPTH, HID, wide), F32) for n in (pairs0, pairs1)]
        + [pltpu.VMEM((n, DEPTH, HID, wide), F32) for n in (pairs0, pairs1)]
        + [
            pltpu.VMEM((2 * HID, 2 * HID), F32),
            pltpu.VMEM((DEPTH, 2 * HID, 32), F32),
            pltpu.VMEM((HID, wide), F32),
        ]
    )
    final, grad, sums = call(
        functools.partial(steps_kernel, rows),
        [shape(8 * rows, LANES), shape(8 * rows, LANES), shape(HID + 8, LANES)],
        [SMEM] + [VMEM] * 8,
        scratch,
        limit=52 * 1024 * 1024,
        flops=10_000_000_000,
    )(b_head, ext, from_west, from_east, a1, w2t, w2, t1, cols_w)

    rounds = [("lat", 1 << b) for b in range(n_lat.bit_length() - 1)]
    rounds += [("lon", 1 << b) for b in range(n_lon.bit_length() - 1)]
    sizes = {"lat": n_lat, "lon": n_lon}
    for number, (axis, bit) in enumerate(rounds):
        other = lax.ppermute(sums, axis, [(i, i ^ bit) for i in range(sizes[axis])])
        if number < len(rounds) - 1:
            sums = sums + other
    scale = 1.0 / math.sqrt(n_lon * cols * n_lat * rows * DEPTH)
    first_grad, second_grad, head_grad = call(
        functools.partial(finish_kernel, scale),
        [shape(6, HID), shape(HID, HID), shape(1, HID)],
        [VMEM] * 2,
    )(sums, other)
    return (
        final.reshape(tracers.shape),
        grad.reshape(tracers.shape),
        first_grad,
        second_grad,
        head_grad.reshape(HID),
    )


def solution(mesh):
    return jax.shard_map(
        per_device,
        mesh=mesh,
        in_specs=(
            P(None, None, "lat", "lon"),
            P("lat", "lon"),
            P("lat", "lon"),
            P("lon"),
            P(None, None, "lat", "lon"),
            P(),
            P(),
            P(),
            P(),
            P(),
            P(),
        ),
        out_specs=(P(None, None, "lat", "lon"), P(None, None, "lat", "lon"), P(), P(), P()),
        check_vma=False,
    )
```

```python
import functools
import math

import jax
import jax.numpy as jnp
from jax import lax
from jax.experimental import pallas as pl
from jax.experimental.pallas import tpu as pltpu
from jax.sharding import PartitionSpec as P

KMAX = 0.24
DEPTH = 4
HID = 128
LANES = 128
HALO = 3
SLOT = 2 * HALO
F32 = jnp.float32
BF16 = jnp.bfloat16


def split(x):
    high = x.astype(BF16)
    low = (x - high.astype(F32)).astype(BF16)
    return high, low


def iota(shape, dim):
    return lax.broadcasted_iota(jnp.int32, shape, dim)


def prepare_kernel(
    rows,
    cols,
    tracer_hbm,
    cot_hbm,
    land_hbm,
    levels_hbm,
    partner_hbm,
    w1_hbm,
    b1_hbm,
    w2_hbm,
    b2_hbm,
    wh_hbm,
    bh_hbm,
    south_first,
    north,
    south_last,
    turn_out,
    offset_out,
    own_out,
    a1_out,
    w2t_out,
    w2_out,
    col_out,
    tracer,
    cot,
    land,
    levels,
    partner,
    w1,
    b1,
    w2,
    b2,
    wh,
    bh,
    sems,
):
    copies = [
        pltpu.make_async_copy(source, target, sems.at[n])
        for n, (source, target) in enumerate(
            (
                (partner_hbm, partner),
                (tracer_hbm, tracer),
                (cot_hbm, cot),
                (land_hbm, land),
                (levels_hbm, levels),
                (w1_hbm, w1),
                (b1_hbm, b1),
                (w2_hbm, w2),
                (b2_hbm, b2),
                (wh_hbm, wh),
                (bh_hbm, bh),
            )
        )
    ]
    for copy in copies:
        copy.start()
    for copy in copies:
        copy.wait()
    here = partner[0]
    n_lon = lax.axis_size("lon")
    turn_out[0] = lax.rem(lax.div(here, cols) + lax.axis_index("lon"), n_lon)
    offset_out[...] = jnp.full((8, LANES), lax.rem(here, cols), jnp.int32)

    at_top = lax.axis_index("lat") == lax.axis_size("lat") - 1
    depth = (land[...] * levels[...]).astype(F32)
    for r in range(rows):
        own_out[24 * r : 24 * r + 8, :] = tracer[pl.ds(r, 8, stride=rows), :]
        own_out[24 * r + 8 : 24 * r + 16, :] = cot[pl.ds(r, 8, stride=rows), :]
        own_out[24 * r + 16 : 24 * r + 24, :] = jnp.broadcast_to(depth[r : r + 1], (8, LANES))

    def edge(first, skip):
        parts = [tracer[pl.ds(first + j, 8, stride=rows), :] for j in range(HALO)]
        parts += [cot[pl.ds(first + skip + j, 8, stride=rows), :] for j in range(2)]
        parts += [depth[first : first + HALO], jnp.zeros((8 - HALO, LANES), F32)]
        return jnp.concatenate(parts, 0)

    low, high = edge(0, 0), edge(rows - HALO, 1)
    south_first[...] = jnp.where(at_top, high, low)
    north[...] = high
    south_last[...] = jnp.where(at_top, low, high)
    prepare_weights(w1, b1, w2, b2, wh, bh, a1_out, w2t_out, w2_out, col_out)


def prepare_weights(w1, b1, w2, b2, wh, bh, a1_out, w2t_out, w2_out, col_out):
    first = w1[...]
    bias_high, bias_low = split(b1[...])
    row = iota((16, LANES), 0)
    pad_row = iota((16, LANES), 0)
    for k in range(DEPTH):
        block = jnp.zeros((16, LANES), F32)
        for t in range(2):
            block = jnp.where(row == t * 4 + k, first[t : t + 1], block)
            if k >= 1:
                block = jnp.where(row == 8 + t * 4 + k - 1, -first[2 + t : 3 + t], block)
            block = jnp.where(row == 8 + t * 4 + k, first[4 + t : 5 + t], block)
        high, low = split(block)
        high32, low32 = high.astype(F32), low.astype(F32)
        tail = jnp.where(
            pad_row == 0,
            bias_high.astype(F32),
            jnp.where(pad_row == 1, bias_low.astype(F32), 0.0),
        )
        tall = jnp.concatenate([high32, high32, low32, tail, jnp.zeros((64, LANES), F32)], 0)
        a1_out[k * HID : (k + 1) * HID, :] = jnp.transpose(tall)[:, :64].astype(BF16)
    second = w2[...]
    for out, matrix in ((w2_out, second), (w2t_out, jnp.transpose(second))):
        high, low = split(matrix)
        out[0:HID, :] = jnp.concatenate([high, high], 1)
        out[HID : 2 * HID, :] = jnp.concatenate([low, low], 1)
    vectors = [b2[...], wh[...]] + [first[f : f + 1] for f in range(6)]
    for n, vector in enumerate(vectors):
        column = jnp.transpose(jnp.broadcast_to(vector, (HID, LANES)))
        col_out[n * HID : (n + 1) * HID, :] = column
    col_out[8 * HID : 8 * HID + 8, :] = jnp.full((8, LANES), bh[0], F32)


def assemble_kernel(rows, offset_in, first, second, third, own, halo, packed):
    lane = iota((8, LANES), 1)
    lat, n_lat = lax.axis_index("lat"), lax.axis_size("lat")
    at_top = lat == n_lat - 1
    below_top = lat == n_lat - 2
    at_bottom = lat == 0
    offset = offset_in[...]
    source = jnp.bitwise_and(offset - lane, LANES - 1)

    def mirrored(place):
        both = jnp.where(
            lane <= offset, first[place : place + 8, :], second[place : place + 8, :]
        )
        return jnp.take_along_axis(both, source, axis=1)

    zero = jnp.zeros((8, LANES), F32)

    def from_north(place):
        return jnp.where(below_top, third[place : place + 8, :], first[place : place + 8, :])

    def from_south(place):
        near = jnp.where(at_top, third[place : place + 8, :], second[place : place + 8, :])
        return jnp.where(at_bottom, 0.0, near)

    def north(plain, folded):
        return jnp.where(at_top, mirrored(folded), from_north(plain))

    def spread(tile, j):
        return jnp.broadcast_to(tile[j : j + 1], (8, LANES))

    depth_south = from_south(40)
    depth_north = from_north(40)
    depth_fold = mirrored(40)
    total = rows + 2 * HALO
    tiles = []
    for i in range(total):
        r = i - HALO
        if r < 0:
            tile_c = from_south(8 * i)
            tile_l = from_south(24 + 8 * (i - 1)) if i >= 1 else zero
            tile_n = spread(depth_south, i)
        elif r < rows:
            tile_c = own[24 * r : 24 * r + 8, :]
            tile_l = own[24 * r + 8 : 24 * r + 16, :]
            tile_n = own[24 * r + 16 : 24 * r + 24, :]
        else:
            j = r - rows
            tile_c = north(8 * j, 8 * (2 - j))
            tile_l = north(24 + 8 * j, 24 + 8 * (1 - j)) if j < 2 else zero
            tile_n = jnp.where(at_top, spread(depth_fold, 2 - j), spread(depth_north, j))
        tiles.append((tile_c, tile_l, tile_n))
        place = 24 * (i if r < 0 else i - rows)
        if not 0 <= r < rows:
            for part, tile in enumerate(tiles[-1]):
                halo[place + 8 * part : place + 8 * part + 8, :] = tile
    for part in range(3):
        acc = zero
        for slot in range(rows + 4):
            moved = pltpu.roll(tiles[slot + 1][part], SLOT * slot + HALO, 1)
            inside = (lane >= SLOT * slot) & (lane < SLOT * slot + SLOT)
            acc = jnp.where(inside, moved, acc)
        packed[8 * part : 8 * part + 8, :] = acc


def steps_kernel(
    rows,
    own_rows,
    halo_rows,
    west_in,
    east_in,
    a1,
    w2t,
    w2,
    cols,
    out_tracer,
    out_grad,
    out_keep,
    out_give,
    c_tiles0,
    c_tiles1,
    wv_tiles,
    wet_tiles,
    kappa_tiles,
    slope0,
    slope1,
    d3_tiles,
    bar_tiles,
    x0,
    x1,
    h1b0,
    h1b1,
    h1f0,
    h1f1,
    h2f0,
    h2f1,
    acc_w2,
    acc_a1,
    acc_head,
):
    total = rows + 2 * HALO
    lane = iota((8, LANES), 1)
    level = jnp.bitwise_and(iota((8, LANES), 0), DEPTH - 1)
    level_wide = jnp.bitwise_and(iota((8, 2 * LANES), 0), DEPTH - 1)
    zero = jnp.zeros((8, LANES), F32)
    side_tile = rows
    tile_of = {i: i - HALO for i in range(HALO, rows + HALO)}
    place = rows + 1
    for ring in (1, 2, 3):
        tile_of[HALO - ring] = place
        tile_of[rows + HALO - 1 + ring] = place + 1
        place += 2
    n_tiles = place + (place % 2)
    slots = range(1, rows + 5)

    def east(main, side):
        return (
            pltpu.roll(jnp.where(lane == 0, side, main), LANES - 1, 1),
            pltpu.roll(jnp.where(lane == 0, main, side), LANES - 1, 1),
        )

    def from_west(main, side):
        return (
            pltpu.roll(jnp.where(lane == LANES - 1, side, main), 1, 1),
            pltpu.roll(jnp.where(lane == LANES - 1, main, side), 1, 1),
        )

    def from_west_main(main, side):
        return pltpu.roll(jnp.where(lane == LANES - 1, side, main), 1, 1)

    def unpack(tile, i):
        return pltpu.roll(tile, LANES - (SLOT * (i - 1) + HALO), 1)

    def pack(tiles):
        acc = zero
        for i, tile in tiles.items():
            slot = i - 1
            moved = pltpu.roll(tile, SLOT * slot + HALO, 1)
            inside = (lane >= SLOT * slot) & (lane < SLOT * slot + SLOT)
            acc = jnp.where(inside, moved, acc)
        return acc

    def column(n):
        part = cols[n * HID : (n + 1) * HID, :]
        return jnp.concatenate([part, part], 1)

    head_bias = cols[8 * HID : 8 * HID + 1, :][:, 0:1]

    def both(x):
        return x + pltpu.roll(x, 4, 0)

    third = lax.rem(lane, SLOT)
    from_left = third < HALO
    side_c_packed = jnp.where(from_left, west_in[0:8, :], east_in[0:8, :])
    side_l_packed = jnp.where(from_left, west_in[8:16, :], east_in[8:16, :])
    side_n_packed = jnp.where(from_left, west_in[16:24, :], east_in[16:24, :])
    side_lanes = (lane < HALO) | (lane >= LANES - HALO)

    def wet_of(depth):
        return jnp.where(depth > level.astype(F32), 1.0, 0.0)

    def vertical_of(depth):
        inside = (depth > (level + 1).astype(F32)) & (level < DEPTH - 1)
        return jnp.where(inside, 1.0, 0.0)

    def tile_at(i, part):
        if HALO <= i < rows + HALO:
            place = 24 * (i - HALO) + 8 * part
            return own_rows[place : place + 8, :]
        place = 24 * (i if i < HALO else i - rows) + 8 * part
        return halo_rows[place : place + 8, :]

    c0, wet = {}, {}
    for i in range(total):
        depth = tile_at(i, 2)
        main_c = tile_at(i, 0)
        main_w = wet_of(depth)
        if i in slots:
            side_c = unpack(side_c_packed, i)
            side_w = jnp.where(side_lanes, wet_of(unpack(side_n_packed, i)), 0.0)
        else:
            side_c, side_w = zero, zero
        c0[i] = (main_c, side_c)
        wet[i] = (main_w, side_w)
        c_tiles0[tile_of[i]] = main_c
        wet_tiles[tile_of[i]] = main_w
        wv_tiles[tile_of[i]] = vertical_of(depth)
    c_tiles0[side_tile] = side_c_packed
    wet_tiles[side_tile] = wet_of(side_n_packed)
    wv_tiles[side_tile] = vertical_of(side_n_packed)
    for tile in range(place, n_tiles):
        c_tiles0[tile] = zero
        wet_tiles[tile] = zero
        wv_tiles[tile] = zero

    def closure(start, steps, group, save, c_tiles, slope, xs, h1b, h1f, h2f):
        def body(step, carry):
            first_pair = start + step * group
            items = [(first_pair + g, k) for g in range(group) for k in range(DEPTH)]
            inputs = []
            for g in range(group):
                p = first_pair + g
                pieces = []
                for a in range(2):
                    c = c_tiles[2 * p + a]
                    v = (pltpu.roll(c, 7, 0) - c) * wv_tiles[2 * p + a]
                    pieces.append(jnp.concatenate([c, v], 0))
                high, low = split(jnp.concatenate(pieces, 1))
                x = jnp.concatenate([high, low, high, jnp.ones((16, 2 * LANES), BF16)], 0)
                if save:
                    xs[p] = x
                inputs.append(jnp.dot(a1[...], x, preferred_element_type=F32))
            outs = [jnp.zeros((8, 2 * LANES), F32)] * group
            pairs = {}
            for j in range(len(items) + 1):
                if j < len(items):
                    p, k = items[j]
                    h1 = jnp.tanh(inputs[j // DEPTH][k * HID : (k + 1) * HID])
                    pairs[j] = jnp.concatenate(split(h1), 0)
                    if save:
                        h1f[p, k] = h1
                        h1b[p, k] = pairs[j]
                if j >= 1:
                    p, k = items[j - 1]
                    z = jnp.dot(w2t[...], pairs.pop(j - 1), preferred_element_type=F32)
                    h2 = jnp.tanh(z[:HID] + z[HID:] + column(0))
                    if save:
                        h2f[p, k] = h2
                    head = jnp.sum(h2 * column(1), 0, keepdims=True)
                    g = (j - 1) // DEPTH
                    outs[g] = jnp.where(level_wide == k, head, outs[g])
            for g in range(group):
                sig = jax.nn.sigmoid(outs[g] + head_bias)
                for a in range(2):
                    tile = 2 * (first_pair + g) + a
                    part = sig[:, a * LANES : (a + 1) * LANES]
                    kappa = KMAX * part * wet_tiles[tile]
                    kappa_tiles[tile] = kappa
                    slope[tile] = kappa * (1.0 - part)
            return carry

        lax.fori_loop(0, steps, body, 0)

    def edge_masks(i):
        east_w = east(*wet[i])
        return tuple(0.5 * a * b for a, b in zip(wet[i], east_w))

    def north_mask(i):
        return tuple(0.5 * a * b for a, b in zip(wet[i], wet[i + 1]))

    def kappas(lo, hi):
        packed = kappa_tiles[side_tile]
        out = {}
        for i in range(lo, hi + 1):
            side = unpack(packed, i) if i in slots else zero
            out[i] = (kappa_tiles[tile_of[i]], side)
        return out

    def coefficients(kappa, lo, hi):
        ce, cn = {}, {}
        for i in range(lo, hi + 1):
            ke = east(*kappa[i])
            ce[i] = tuple(m * (a + b) for m, a, b in zip(edge_masks(i), kappa[i], ke))
        for i in range(lo - 1, hi + 1):
            cn[i] = tuple(
                m * (a + b) for m, a, b in zip(north_mask(i), kappa[i], kappa[i + 1])
            )
        return ce, cn

    def diffs(field, lo, hi):
        de, dn = {}, {}
        for i in range(lo, hi + 1):
            fe = east(*field[i])
            de[i] = tuple(b - a for a, b in zip(field[i], fe))
        for i in range(lo - 1, hi + 1):
            dn[i] = tuple(b - a for a, b in zip(field[i], field[i + 1]))
        return de, dn

    def diffuse(field, ce, cn, de, dn, lo, hi):
        out = {}
        flux_n = {i: tuple(c * d for c, d in zip(cn[i], dn[i])) for i in range(lo - 1, hi + 1)}
        for i in range(lo, hi + 1):
            fe = tuple(c * d for c, d in zip(ce[i], de[i]))
            fw = from_west(*fe)
            out[i] = tuple(
                f + ((a - b) + (c - d))
                for f, a, b, c, d in zip(field[i], fe, fw, flux_n[i], flux_n[i - 1])
            )
        return out

    def kappa_bars(de, dn, le, ln, lo, hi):
        out = {}
        gn = {}
        for i in range(lo - 1, hi + 1):
            gn[i] = tuple(-m * a * b for m, a, b in zip(north_mask(i), dn[i], ln[i]))
        for i in range(lo, hi + 1):
            ge = tuple(-m * a * b for m, a, b in zip(edge_masks(i), de[i], le[i]))
            gw = from_west(*ge)
            out[i] = tuple(
                both((a + b) + (c + d)) for a, b, c, d in zip(ge, gw, gn[i], gn[i - 1])
            )
        return out

    def outer(left, right):
        return lax.dot_general(
            left, right, (((1,), (1,)), ((), ())), preferred_element_type=F32
        )

    sublane_wide = iota((8, 2 * LANES), 0)

    def groups(x):
        return jnp.sum(x.reshape(HID // 8, 8, 2 * LANES), 0)

    def put_row(bars, n, row, part):
        value = jnp.where(sublane_wide == row, jnp.sum(part, 0, keepdims=True), 0.0)
        bars = list(bars)
        bars[n] = plus(bars[n], value)
        return bars

    def plus(left, right):
        return right if left is None else left + right

    def closure_back(start, steps, group, with_sums, slope, xs, h1b, h1f, h2f):
        def body(step, carry):
            first_pair = start + step * group
            items = [(first_pair + g, k) for g in range(group) for k in range(DEPTH)]
            d3 = [
                jnp.concatenate(
                    [
                        d3_tiles[2 * (first_pair + g) + a] * slope[2 * (first_pair + g) + a]
                        for a in range(2)
                    ],
                    1,
                )
                for g in range(group)
            ]
            bars = [[None] * 6 for g in range(group)]
            sum_w2, sum_head, sum_a1 = None, None, None
            seconds, firsts = {}, {}
            for j in range(len(items) + 2):
                if j < len(items):
                    p, k = items[j]
                    h2 = h2f[p, k]
                    row = d3[j // DEPTH][k : k + 1]
                    d2 = (column(1) * row) * (1.0 - h2 * h2)
                    seconds[j] = jnp.concatenate(split(d2), 0)
                    if with_sums:
                        sum_head = plus(sum_head, h2 * row)
                if 1 <= j <= len(items):
                    p, k = items[j - 1]
                    d2b = seconds.pop(j - 1)
                    e = jnp.dot(w2[...], d2b, preferred_element_type=F32)
                    h1 = h1f[p, k]
                    d1 = (e[:HID] + e[HID:]) * (1.0 - h1 * h1)
                    firsts[j - 1] = d1
                    if with_sums:
                        sum_w2 = plus(sum_w2, outer(h1b[p, k], d2b))
                if j >= 2:
                    p, k = items[j - 2]
                    g = (j - 2) // DEPTH
                    d1 = firsts.pop(j - 2)
                    if with_sums:
                        seconds[g, k] = jnp.concatenate(split(d1), 0)
                        if k == DEPTH - 1:
                            d1b = jnp.concatenate([seconds.pop((g, n)) for n in range(DEPTH)], 0)
                            sum_a1 = plus(sum_a1, outer(d1b, xs[p, 0:32, :]))
                    parts = [groups(d1 * column(2 + f)) for f in range(6)]
                    for t in range(2):
                        bars[g] = put_row(bars[g], t, t * DEPTH + k, parts[t])
                        if k >= 1:
                            below = bars[g][2 + t]
                            bars[g] = put_row(
                                bars[g], 4 + t, t * DEPTH + k - 1, below - parts[2 + t]
                            )
                        bars[g][2 + t] = parts[4 + t]
            if with_sums:
                acc_w2[...] += sum_w2
                acc_head[...] += sum_head
                acc_a1[...] += sum_a1
            for g in range(group):
                cells = plus(bars[g][0], bars[g][1])
                vertical = plus(bars[g][4], bars[g][5])
                for a in range(2):
                    tile = 2 * (first_pair + g) + a
                    lanes = slice(a * LANES, (a + 1) * LANES)
                    v = vertical[:, lanes] * wv_tiles[tile]
                    bar_tiles[tile] = cells[:, lanes] - v + pltpu.roll(v, 1, 0)
            return carry

        lax.fori_loop(0, steps, body, 0)

    low, high = HALO, rows + HALO - 1
    step0 = (c_tiles0, slope0, x0, h1b0, h1f0, h2f0)
    own = rows // 2
    closure(0, own // 4, 4, True, *step0)
    closure(own, (n_tiles // 2 - own) // 2, 2, False, *step0)
    kappa0 = kappas(0, total - 1)
    ce0, cn0 = coefficients(kappa0, low - 2, high + 2)
    de0, dn0 = diffs(c0, low - 2, high + 2)
    c1 = diffuse(c0, ce0, cn0, de0, dn0, low - 2, high + 2)
    for i in range(low - 2, high + 3):
        c_tiles1[tile_of[i]] = c1[i][0]
    c_tiles1[side_tile] = pack({i: c1[i][1] for i in range(low - 2, high + 3)})
    tiles1 = rows + 5
    for tile in range(tiles1, n_tiles):
        c_tiles1[tile] = zero
    step1 = (c_tiles1, slope1, x1, h1b1, h1f1, h2f1)
    closure(0, own // 4, 4, True, *step1)
    closure(own, 1, 2, True, *step1)
    closure(own + 2, 1, 1, False, *step1)
    kappa1 = kappas(low - 2, high + 2)
    ce1, cn1 = coefficients(kappa1, low - 1, high + 1)
    de1, dn1 = diffs(c1, low - 1, high + 1)
    c2 = diffuse(c1, ce1, cn1, de1, dn1, low, high)
    for i in range(low, high + 1):
        out_tracer[pl.ds(i - low, 8, stride=rows), :] = c2[i][0]
    lam2 = {}
    for i in range(low - 2, high + 3):
        lam2[i] = (tile_at(i, 1), unpack(side_l_packed, i))
    le, ln = diffs(lam2, low - 1, high + 1)
    direct = diffuse(lam2, ce1, cn1, le, ln, low - 1, high + 1)
    bars = kappa_bars(de1, dn1, le, ln, low - 1, high + 1)
    for i in range(low - 1, high + 2):
        d3_tiles[tile_of[i]] = bars[i][0]
    d3_tiles[side_tile] = pack({i: bars[i][1] for i in range(low, high + 1)})
    d3_tiles[rows + 3] = zero
    acc_w2[...] = jnp.zeros_like(acc_w2)
    acc_a1[...] = jnp.zeros_like(acc_a1)
    acc_head[...] = jnp.zeros_like(acc_head)
    closure_back(0, own // 4, 4, True, *step1[1:])
    closure_back(own, 1, 2, False, *step1[1:])
    side_bar = bar_tiles[side_tile]
    lam1 = {}
    for i in range(low - 1, high + 2):
        main = direct[i][0] + bar_tiles[tile_of[i]]
        side = direct[i][1] + unpack(side_bar, i)
        lam1[i] = (main, side)
    le, ln = diffs(lam1, low, high)
    direct = diffuse(lam1, ce0, cn0, le, ln, low, high)
    bars = kappa_bars(de0, dn0, le, ln, low, high)
    for i in range(low, high + 1):
        d3_tiles[tile_of[i]] = bars[i][0]
    closure_back(0, own // 4, 4, True, *step0[1:])
    for i in range(low, high + 1):
        out_grad[pl.ds(i - low, 8, stride=rows), :] = direct[i][0] + bar_tiles[tile_of[i]]
    first = [None] * 6

    def add(f, value):
        first[f] = value if first[f] is None else first[f] + value

    for k in range(DEPTH):
        cells = acc_a1[2 * HID * k : 2 * HID * k + HID, :]
        cells = cells + acc_a1[2 * HID * k + HID : 2 * HID * (k + 1), :]
        cells = jnp.concatenate([cells, jnp.zeros((HID, LANES - 32), F32)], 1)
        turned = jnp.transpose(cells)
        turned = turned[0:16] + turned[16:32]
        for t in range(2):
            add(t, turned[t * 4 + k : t * 4 + k + 1])
            if k >= 1:
                add(2 + t, -turned[8 + t * 4 + k - 1 : 8 + t * 4 + k])
            add(4 + t, turned[8 + t * 4 + k : 8 + t * 4 + k + 1])
    head = jnp.sum(jnp.transpose(acc_head[:, :LANES] + acc_head[:, LANES:]), 0, keepdims=True)
    rest = jnp.concatenate(first + [head, jnp.zeros_like(head)], 0)
    second = (acc_w2[:HID, :HID] + acc_w2[HID:, HID:]) + (acc_w2[:HID, HID:] + acc_w2[HID:, :HID])
    odd = jnp.bitwise_and(lax.axis_index("lat"), 1) == 1
    left, right = second[: HID // 2], second[HID // 2 :]
    out_keep[0 : HID // 2, :] = jnp.where(odd, right, left)
    out_give[0 : HID // 2, :] = jnp.where(odd, left, right)
    out_keep[HID // 2 :, :] = jnp.where(odd, 0.0, rest)
    out_give[HID // 2 :, :] = jnp.where(odd, rest, 0.0)


def finish_kernel(scale, mine, other, w1_out, w2_out, wh_out):
    odd = jnp.bitwise_and(lax.axis_index("lat"), 1) == 1
    half = HID // 2
    a, b = mine[...], other[...]
    left, right = jnp.where(odd, b, a) * scale, jnp.where(odd, a, b) * scale
    w2_out[0:half, :] = left[:half]
    w2_out[half:, :] = right[:half]
    w1_out[...] = left[half : half + 6]
    wh_out[...] = left[half + 6 : half + 7]


VMEM = pl.BlockSpec(memory_space=pltpu.VMEM)
SMEM = pl.BlockSpec(memory_space=pltpu.SMEM)
HBM = pl.BlockSpec(memory_space=pltpu.HBM)


def call(kernel, outs, ins, out_specs=None, scratch=(), limit=4 * 1024 * 1024, flops=1_000_000, size=1_000_000):
    return pl.pallas_call(
        kernel,
        out_shape=outs,
        in_specs=ins,
        out_specs=out_specs or [VMEM] * len(outs),
        scratch_shapes=list(scratch),
        compiler_params=pltpu.CompilerParams(vmem_limit_bytes=limit),
        cost_estimate=pl.CostEstimate(flops=flops, bytes_accessed=size, transcendentals=0),
    )


def shape(*dims, dtype=F32):
    return jax.ShapeDtypeStruct(dims, dtype)


def per_device(
    tracers,
    land_mask,
    level_counts,
    fold_partner,
    cotangent,
    w_first,
    b_first,
    w_second,
    b_second,
    w_head,
    b_head,
):
    rows, cols = land_mask.shape
    n_lon, n_lat = lax.axis_size("lon"), lax.axis_size("lat")
    tracer2 = tracers.reshape(8 * rows, cols)
    cot2 = cotangent.reshape(8 * rows, cols)

    args = (
        tracer2,
        cot2,
        land_mask,
        level_counts,
        fold_partner,
        w_first,
        b_first.reshape(1, HID),
        w_second,
        b_second.reshape(1, HID),
        w_head.reshape(1, HID),
        b_head,
    )
    spaces = [pltpu.SMEM if x is fold_partner or x is b_head else pltpu.VMEM for x in args]
    south_first, north, south_last, turn, offset, own_rows, a1, w2t, w2, cols_w = call(
        functools.partial(prepare_kernel, rows, cols),
        [shape(48, LANES)] * 3
        + [
            shape(1, dtype=jnp.int32),
            shape(8, LANES, dtype=jnp.int32),
            shape(24 * rows, LANES),
            shape(DEPTH * HID, 64, dtype=BF16),
            shape(2 * HID, 2 * HID, dtype=BF16),
            shape(2 * HID, 2 * HID, dtype=BF16),
            shape(8 * HID + 8, LANES),
        ],
        [HBM] * len(args),
        out_specs=[VMEM] * 3 + [SMEM] + [VMEM] * 6,
        limit=None,
        scratch=[space(x.shape, x.dtype) for space, x in zip(spaces, args)]
        + [pltpu.SemaphoreType.DMA((len(args),))],
    )(*args)

    def exchange(j, first, second, third):
        top = n_lat - 1

        def send(x, plain, fold):
            pairs = [
                (b * n_lat + source, b * n_lat + target)
                for b in range(n_lon)
                for source, target in plain
            ]
            if fold is not None:
                pairs += [
                    (b * n_lat + top, ((fold - b) % n_lon) * n_lat + top) for b in range(n_lon)
                ]
            return lax.ppermute(x, ("lon", "lat"), pairs)

        south = [(i + 1, i) for i in range(top - 1)] + [(0, top - 1)]
        north = [(i, i + 1) for i in range(top - 1)] + [(top - 1, 0)]
        last = [(i, i ^ 1) for i in range(n_lat)]
        return send(first, south, j), send(second, north, j - 1), send(third, last, None)

    from_first, from_second, from_third = lax.switch(
        turn[0],
        [functools.partial(exchange, j) for j in range(n_lon)],
        south_first,
        north,
        south_last,
    )

    total = rows + 2 * HALO
    halo_rows, packed = call(
        functools.partial(assemble_kernel, rows),
        [shape(24 * 2 * HALO, LANES), shape(24, LANES)],
        [VMEM] * 5,
    )(offset, from_first, from_second, from_third, own_rows)
    from_west = lax.ppermute(packed, "lon", [(i, (i + 1) % n_lon) for i in range(n_lon)])
    from_east = lax.ppermute(packed, "lon", [((i + 1) % n_lon, i) for i in range(n_lon)])

    n_tiles = total + 1 + (total + 1) % 2
    pairs0 = rows // 2
    pairs1 = rows // 2 + 2
    tiles = pltpu.VMEM((n_tiles, 8, LANES), F32)
    wide = 2 * LANES
    scratch = (
        [tiles] * 9
        + [pltpu.VMEM((n, 64, wide), BF16) for n in (pairs0, pairs1)]
        + [pltpu.VMEM((n, DEPTH, 2 * HID, wide), BF16) for n in (pairs0, pairs1)]
        + [pltpu.VMEM((n, DEPTH, HID, wide), F32) for n in (pairs0, pairs1)]
        + [pltpu.VMEM((n, DEPTH, HID, wide), F32) for n in (pairs0, pairs1)]
        + [
            pltpu.VMEM((2 * HID, 2 * HID), F32),
            pltpu.VMEM((DEPTH * 2 * HID, 32), F32),
            pltpu.VMEM((HID, wide), F32),
        ]
    )
    final, grad, keep, give = call(
        functools.partial(steps_kernel, rows),
        [shape(8 * rows, LANES)] * 2 + [shape(HID // 2 + 8, LANES)] * 2,
        [VMEM] * 8,
        scratch=scratch,
        limit=36 * 1024 * 1024,
        flops=10_000_000_000,
    )(own_rows, halo_rows, from_west, from_east, a1, w2t, w2, cols_w)

    def swap(x, mask):
        pairs = [(i, i ^ mask) for i in range(n_lon * n_lat)]
        return lax.ppermute(x, ("lon", "lat"), pairs)

    sums = keep + swap(give, 1)
    bits = [1 << b for b in range(1, (n_lon * n_lat).bit_length() - 1)]
    while bits:
        a, bits = bits[0], bits[1:]
        if bits:
            b, bits = bits[0], bits[1:]
            near, far, both = swap(sums, a), swap(sums, b), swap(sums, a | b)
            sums = (sums + near) + (far + both)
        else:
            sums = sums + swap(sums, a)
    other = swap(sums, 1)
    scale = 1.0 / math.sqrt(n_lon * cols * n_lat * rows * DEPTH)
    first_grad, second_grad, head_grad = call(
        functools.partial(finish_kernel, scale),
        [shape(6, HID), shape(HID, HID), shape(1, HID)],
        [VMEM] * 2,
    )(sums, other)
    return (
        final.reshape(tracers.shape),
        grad.reshape(tracers.shape),
        first_grad,
        second_grad,
        head_grad.reshape(HID),
    )


def solution(mesh):
    return jax.shard_map(
        per_device,
        mesh=mesh,
        in_specs=(
            P(None, None, "lat", "lon"),
            P("lat", "lon"),
            P("lat", "lon"),
            P("lon"),
            P(None, None, "lat", "lon"),
            P(),
            P(),
            P(),
            P(),
            P(),
            P(),
        ),
        out_specs=(P(None, None, "lat", "lon"), P(None, None, "lat", "lon"), P(), P(), P()),
        check_vma=False,
    )
```

```python
import functools
import math

import jax
import jax.numpy as jnp
from jax import lax
from jax.experimental import pallas as pl
from jax.experimental.pallas import tpu as pltpu
from jax.sharding import PartitionSpec as P

KMAX = 0.24
DEPTH = 4
HID = 128
LANES = 128
HALO = 3
SLOT = 2 * HALO
F32 = jnp.float32
BF16 = jnp.bfloat16


def split(x):
    high = x.astype(BF16)
    low = (x - high.astype(F32)).astype(BF16)
    return high, low


def iota(shape, dim):
    return lax.broadcasted_iota(jnp.int32, shape, dim)


def edges_kernel(
    rows,
    cols,
    tracer_hbm,
    cot_hbm,
    land_hbm,
    levels_hbm,
    partner_hbm,
    south_first,
    north,
    south_last,
    turn_out,
    tracer,
    cot,
    land,
    levels,
    partner,
    sems,
):
    pairs = (
        (partner_hbm, partner),
        (tracer_hbm, tracer),
        (cot_hbm, cot),
        (land_hbm, land),
        (levels_hbm, levels),
    )
    copies = [
        pltpu.make_async_copy(source, target, sems.at[n])
        for n, (source, target) in enumerate(pairs)
    ]
    for copy in copies:
        copy.start()
    for copy in copies:
        copy.wait()
    turn_out[0] = lax.rem(lax.div(partner[0], cols) + lax.axis_index("lon"), lax.axis_size("lon"))

    at_top = lax.axis_index("lat") == lax.axis_size("lat") - 1
    depth = (land[...] * levels[...]).astype(F32)

    def edge(first, skip):
        parts = [tracer[pl.ds(first + j, 8, stride=rows), :] for j in range(HALO)]
        parts += [cot[pl.ds(first + skip + j, 8, stride=rows), :] for j in range(2)]
        parts += [depth[first : first + HALO], jnp.zeros((8 - HALO, LANES), F32)]
        return jnp.concatenate(parts, 0)

    low, high = edge(0, 0), edge(rows - HALO, 1)
    south_first[...] = jnp.where(at_top, high, low)
    north[...] = high
    south_last[...] = jnp.where(at_top, low, high)


def weights_kernel(w1, b1, w2, b2, wh, bh, a1_out, w2t_out, w2_out, col_out):
    first = w1[...]
    bias_high, bias_low = split(b1[...])
    row = iota((16, LANES), 0)
    pad_row = iota((16, LANES), 0)
    for k in range(DEPTH):
        block = jnp.zeros((16, LANES), F32)
        for t in range(2):
            block = jnp.where(row == t * 4 + k, first[t : t + 1], block)
            if k >= 1:
                block = jnp.where(row == 8 + t * 4 + k - 1, -first[2 + t : 3 + t], block)
            block = jnp.where(row == 8 + t * 4 + k, first[4 + t : 5 + t], block)
        high, low = split(block)
        high32, low32 = high.astype(F32), low.astype(F32)
        tail = jnp.where(
            pad_row == 0,
            bias_high.astype(F32),
            jnp.where(pad_row == 1, bias_low.astype(F32), 0.0),
        )
        tall = jnp.concatenate([high32, high32, low32, tail, jnp.zeros((64, LANES), F32)], 0)
        a1_out[k * HID : (k + 1) * HID, :] = jnp.transpose(tall)[:, :64].astype(BF16)
    second = w2[...]
    for out, matrix in ((w2_out, second), (w2t_out, jnp.transpose(second))):
        high, low = split(matrix)
        out[0:HID, :] = jnp.concatenate([high, high], 1)
        out[HID : 2 * HID, :] = jnp.concatenate([low, low], 1)
    vectors = [b2[...], wh[...]] + [first[f : f + 1] for f in range(6)]
    for n, vector in enumerate(vectors):
        column = jnp.transpose(jnp.broadcast_to(vector, (HID, LANES)))
        col_out[n * HID : (n + 1) * HID, :] = column
    col_out[8 * HID : 8 * HID + 8, :] = jnp.broadcast_to(bh[...], (8, LANES))


def assemble_kernel(
    rows, partner, first, second, third, tracer, cot, land, levels, ext, packed
):
    lane = iota((8, LANES), 1)
    lat, n_lat = lax.axis_index("lat"), lax.axis_size("lat")
    at_top = lat == n_lat - 1
    below_top = lat == n_lat - 2
    at_bottom = lat == 0
    source = jnp.broadcast_to(jnp.bitwise_and(partner[...], LANES - 1), (8, LANES))
    offset = jnp.broadcast_to(source[:, 0:1], (8, LANES))

    def mirrored(place):
        both = jnp.where(
            lane <= offset, first[place : place + 8, :], second[place : place + 8, :]
        )
        return jnp.take_along_axis(both, source, axis=1)

    zero = jnp.zeros((8, LANES), F32)

    def from_north(place):
        return jnp.where(below_top, third[place : place + 8, :], first[place : place + 8, :])

    def from_south(place):
        near = jnp.where(at_top, third[place : place + 8, :], second[place : place + 8, :])
        return jnp.where(at_bottom, 0.0, near)

    def north(plain, folded):
        return jnp.where(at_top, mirrored(folded), from_north(plain))

    def spread(tile, j):
        return jnp.broadcast_to(tile[j : j + 1], (8, LANES))

    depth_here = (land[...] * levels[...]).astype(F32)
    depth_south = from_south(40)
    depth_north = from_north(40)
    depth_fold = mirrored(40)
    total = rows + 2 * HALO
    tiles = []
    for i in range(total):
        r = i - HALO
        if r < 0:
            tile_c = from_south(8 * i)
            tile_l = from_south(24 + 8 * (i - 1)) if i >= 1 else zero
            tile_n = spread(depth_south, i)
        elif r < rows:
            tile_c = tracer[pl.ds(r, 8, stride=rows), :]
            tile_l = cot[pl.ds(r, 8, stride=rows), :]
            tile_n = spread(depth_here, r)
        else:
            j = r - rows
            tile_c = north(8 * j, 8 * (2 - j))
            tile_l = north(24 + 8 * j, 24 + 8 * (1 - j)) if j < 2 else zero
            tile_n = jnp.where(at_top, spread(depth_fold, 2 - j), spread(depth_north, j))
        tiles.append((tile_c, tile_l, tile_n))
        for part, tile in enumerate(tiles[-1]):
            ext[24 * i + 8 * part : 24 * i + 8 * part + 8, :] = tile
    for part in range(3):
        acc = zero
        for slot in range(rows + 4):
            moved = pltpu.roll(tiles[slot + 1][part], SLOT * slot + HALO, 1)
            inside = (lane >= SLOT * slot) & (lane < SLOT * slot + SLOT)
            acc = jnp.where(inside, moved, acc)
        packed[8 * part : 8 * part + 8, :] = acc


def steps_kernel(
    rows,
    ext,
    west_in,
    east_in,
    a1,
    w2t,
    w2,
    cols,
    out_tracer,
    out_grad,
    out_keep,
    out_give,
    c_tiles0,
    c_tiles1,
    wv_tiles,
    wet_tiles,
    kappa_tiles,
    slope0,
    slope1,
    d3_tiles,
    bar_tiles,
    x0,
    x1,
    h1b0,
    h1b1,
    h1f0,
    h1f1,
    h2f0,
    h2f1,
    acc_w2,
    acc_a1,
    acc_head,
):
    total = rows + 2 * HALO
    lane = iota((8, LANES), 1)
    level = jnp.bitwise_and(iota((8, LANES), 0), DEPTH - 1)
    level_wide = jnp.bitwise_and(iota((8, 2 * LANES), 0), DEPTH - 1)
    zero = jnp.zeros((8, LANES), F32)
    side_tile = rows
    tile_of = {i: i - HALO for i in range(HALO, rows + HALO)}
    place = rows + 1
    for ring in (1, 2, 3):
        tile_of[HALO - ring] = place
        tile_of[rows + HALO - 1 + ring] = place + 1
        place += 2
    n_tiles = place + (place % 2)
    slots = range(1, rows + 5)

    def east(main, side):
        return (
            pltpu.roll(jnp.where(lane == 0, side, main), LANES - 1, 1),
            pltpu.roll(jnp.where(lane == 0, main, side), LANES - 1, 1),
        )

    def from_west(main, side):
        return (
            pltpu.roll(jnp.where(lane == LANES - 1, side, main), 1, 1),
            pltpu.roll(jnp.where(lane == LANES - 1, main, side), 1, 1),
        )

    def from_west_main(main, side):
        return pltpu.roll(jnp.where(lane == LANES - 1, side, main), 1, 1)

    def unpack(tile, i):
        return pltpu.roll(tile, LANES - (SLOT * (i - 1) + HALO), 1)

    def pack(tiles):
        acc = zero
        for i, tile in tiles.items():
            slot = i - 1
            moved = pltpu.roll(tile, SLOT * slot + HALO, 1)
            inside = (lane >= SLOT * slot) & (lane < SLOT * slot + SLOT)
            acc = jnp.where(inside, moved, acc)
        return acc

    def column(n):
        part = cols[n * HID : (n + 1) * HID, :]
        return jnp.concatenate([part, part], 1)

    head_bias = cols[8 * HID : 8 * HID + 1, :][:, 0:1]

    def both(x):
        return x + pltpu.roll(x, 4, 0)

    third = lax.rem(lane, SLOT)
    from_left = third < HALO
    side_c_packed = jnp.where(from_left, west_in[0:8, :], east_in[0:8, :])
    side_l_packed = jnp.where(from_left, west_in[8:16, :], east_in[8:16, :])
    side_n_packed = jnp.where(from_left, west_in[16:24, :], east_in[16:24, :])
    side_lanes = (lane < HALO) | (lane >= LANES - HALO)

    def wet_of(depth):
        return jnp.where(depth > level.astype(F32), 1.0, 0.0)

    def vertical_of(depth):
        inside = (depth > (level + 1).astype(F32)) & (level < DEPTH - 1)
        return jnp.where(inside, 1.0, 0.0)

    def tile_at(i, part):
        place = 24 * i + 8 * part
        return ext[place : place + 8, :]

    c0, wet = {}, {}
    for i in range(total):
        depth = tile_at(i, 2)
        main_c = tile_at(i, 0)
        main_w = wet_of(depth)
        if i in slots:
            side_c = unpack(side_c_packed, i)
            side_w = jnp.where(side_lanes, wet_of(unpack(side_n_packed, i)), 0.0)
        else:
            side_c, side_w = zero, zero
        c0[i] = (main_c, side_c)
        wet[i] = (main_w, side_w)
        c_tiles0[tile_of[i]] = main_c
        wet_tiles[tile_of[i]] = main_w
        wv_tiles[tile_of[i]] = vertical_of(depth)
    c_tiles0[side_tile] = side_c_packed
    wet_tiles[side_tile] = wet_of(side_n_packed)
    wv_tiles[side_tile] = vertical_of(side_n_packed)
    for tile in range(place, n_tiles):
        c_tiles0[tile] = zero
        wet_tiles[tile] = zero
        wv_tiles[tile] = zero

    def closure(start, steps, group, save, c_tiles, slope, xs, h1b, h1f, h2f):
        def body(step, carry):
            first_pair = start + step * group
            items = [(first_pair + g, k) for g in range(group) for k in range(DEPTH)]
            inputs = []
            for g in range(group):
                p = first_pair + g
                pieces = []
                for a in range(2):
                    c = c_tiles[2 * p + a]
                    v = (pltpu.roll(c, 7, 0) - c) * wv_tiles[2 * p + a]
                    pieces.append(jnp.concatenate([c, v], 0))
                high, low = split(jnp.concatenate(pieces, 1))
                x = jnp.concatenate([high, low, high, jnp.ones((16, 2 * LANES), BF16)], 0)
                if save:
                    xs[p] = x
                inputs.append(jnp.dot(a1[...], x, preferred_element_type=F32))
            outs = [jnp.zeros((8, 2 * LANES), F32)] * group
            pairs = {}
            for j in range(len(items) + 1):
                if j < len(items):
                    p, k = items[j]
                    h1 = jnp.tanh(inputs[j // DEPTH][k * HID : (k + 1) * HID])
                    pairs[j] = jnp.concatenate(split(h1), 0)
                    if save:
                        h1f[p, k] = h1
                        h1b[p, k] = pairs[j]
                if j >= 1:
                    p, k = items[j - 1]
                    z = jnp.dot(w2t[...], pairs.pop(j - 1), preferred_element_type=F32)
                    h2 = jnp.tanh(z[:HID] + z[HID:] + column(0))
                    if save:
                        h2f[p, k] = h2
                    head = jnp.sum(h2 * column(1), 0, keepdims=True)
                    g = (j - 1) // DEPTH
                    outs[g] = jnp.where(level_wide == k, head, outs[g])
            for g in range(group):
                sig = jax.nn.sigmoid(outs[g] + head_bias)
                for a in range(2):
                    tile = 2 * (first_pair + g) + a
                    part = sig[:, a * LANES : (a + 1) * LANES]
                    kappa = KMAX * part * wet_tiles[tile]
                    kappa_tiles[tile] = kappa
                    slope[tile] = kappa * (1.0 - part)
            return carry

        lax.fori_loop(0, steps, body, 0)

    def edge_masks(i):
        east_w = east(*wet[i])
        return tuple(0.5 * a * b for a, b in zip(wet[i], east_w))

    def north_mask(i):
        return tuple(0.5 * a * b for a, b in zip(wet[i], wet[i + 1]))

    def kappas(lo, hi):
        packed = kappa_tiles[side_tile]
        out = {}
        for i in range(lo, hi + 1):
            side = unpack(packed, i) if i in slots else zero
            out[i] = (kappa_tiles[tile_of[i]], side)
        return out

    def coefficients(kappa, lo, hi):
        ce, cn = {}, {}
        for i in range(lo, hi + 1):
            ke = east(*kappa[i])
            ce[i] = tuple(m * (a + b) for m, a, b in zip(edge_masks(i), kappa[i], ke))
        for i in range(lo - 1, hi + 1):
            cn[i] = tuple(
                m * (a + b) for m, a, b in zip(north_mask(i), kappa[i], kappa[i + 1])
            )
        return ce, cn

    def diffs(field, lo, hi):
        de, dn = {}, {}
        for i in range(lo, hi + 1):
            fe = east(*field[i])
            de[i] = tuple(b - a for a, b in zip(field[i], fe))
        for i in range(lo - 1, hi + 1):
            dn[i] = tuple(b - a for a, b in zip(field[i], field[i + 1]))
        return de, dn

    def diffuse(field, ce, cn, de, dn, lo, hi):
        out = {}
        flux_n = {i: tuple(c * d for c, d in zip(cn[i], dn[i])) for i in range(lo - 1, hi + 1)}
        for i in range(lo, hi + 1):
            fe = tuple(c * d for c, d in zip(ce[i], de[i]))
            fw = from_west(*fe)
            out[i] = tuple(
                f + ((a - b) + (c - d))
                for f, a, b, c, d in zip(field[i], fe, fw, flux_n[i], flux_n[i - 1])
            )
        return out

    def kappa_bars(de, dn, le, ln, lo, hi):
        out = {}
        gn = {}
        for i in range(lo - 1, hi + 1):
            gn[i] = tuple(-m * a * b for m, a, b in zip(north_mask(i), dn[i], ln[i]))
        for i in range(lo, hi + 1):
            ge = tuple(-m * a * b for m, a, b in zip(edge_masks(i), de[i], le[i]))
            gw = from_west(*ge)
            out[i] = tuple(
                both((a + b) + (c + d)) for a, b, c, d in zip(ge, gw, gn[i], gn[i - 1])
            )
        return out

    def outer(left, right):
        return lax.dot_general(
            left, right, (((1,), (1,)), ((), ())), preferred_element_type=F32
        )

    sublane_wide = iota((8, 2 * LANES), 0)

    def groups(x):
        return jnp.sum(x.reshape(HID // 8, 8, 2 * LANES), 0)

    def put_row(bars, n, row, part):
        value = jnp.where(sublane_wide == row, jnp.sum(part, 0, keepdims=True), 0.0)
        bars = list(bars)
        bars[n] = plus(bars[n], value)
        return bars

    def plus(left, right):
        return right if left is None else left + right

    def closure_back(start, steps, group, with_sums, slope, xs, h1b, h1f, h2f):
        def body(step, carry):
            first_pair = start + step * group
            items = [(first_pair + g, k) for g in range(group) for k in range(DEPTH)]
            d3 = [
                jnp.concatenate(
                    [
                        d3_tiles[2 * (first_pair + g) + a] * slope[2 * (first_pair + g) + a]
                        for a in range(2)
                    ],
                    1,
                )
                for g in range(group)
            ]
            bars = [[None] * 6 for g in range(group)]
            sum_w2, sum_head, sum_a1 = None, None, None
            seconds, firsts = {}, {}
            for j in range(len(items) + 2):
                if j < len(items):
                    p, k = items[j]
                    h2 = h2f[p, k]
                    row = d3[j // DEPTH][k : k + 1]
                    d2 = (column(1) * row) * (1.0 - h2 * h2)
                    seconds[j] = jnp.concatenate(split(d2), 0)
                    if with_sums:
                        sum_head = plus(sum_head, h2 * row)
                if 1 <= j <= len(items):
                    p, k = items[j - 1]
                    d2b = seconds.pop(j - 1)
                    e = jnp.dot(w2[...], d2b, preferred_element_type=F32)
                    h1 = h1f[p, k]
                    d1 = (e[:HID] + e[HID:]) * (1.0 - h1 * h1)
                    firsts[j - 1] = d1
                    if with_sums:
                        sum_w2 = plus(sum_w2, outer(h1b[p, k], d2b))
                if j >= 2:
                    p, k = items[j - 2]
                    g = (j - 2) // DEPTH
                    d1 = firsts.pop(j - 2)
                    if with_sums:
                        seconds[g, k] = jnp.concatenate(split(d1), 0)
                        if k == DEPTH - 1:
                            d1b = jnp.concatenate([seconds.pop((g, n)) for n in range(DEPTH)], 0)
                            sum_a1 = plus(sum_a1, outer(d1b, xs[p, 0:32, :]))
                    parts = [groups(d1 * column(2 + f)) for f in range(6)]
                    for t in range(2):
                        bars[g] = put_row(bars[g], t, t * DEPTH + k, parts[t])
                        if k >= 1:
                            below = bars[g][2 + t]
                            bars[g] = put_row(
                                bars[g], 4 + t, t * DEPTH + k - 1, below - parts[2 + t]
                            )
                        bars[g][2 + t] = parts[4 + t]
            if with_sums:
                acc_w2[...] += sum_w2
                acc_head[...] += sum_head
                acc_a1[...] += sum_a1
            for g in range(group):
                cells = plus(bars[g][0], bars[g][1])
                vertical = plus(bars[g][4], bars[g][5])
                for a in range(2):
                    tile = 2 * (first_pair + g) + a
                    lanes = slice(a * LANES, (a + 1) * LANES)
                    v = vertical[:, lanes] * wv_tiles[tile]
                    bar_tiles[tile] = cells[:, lanes] - v + pltpu.roll(v, 1, 0)
            return carry

        lax.fori_loop(0, steps, body, 0)

    low, high = HALO, rows + HALO - 1
    step0 = (c_tiles0, slope0, x0, h1b0, h1f0, h2f0)
    own = rows // 2
    closure(0, own // 4, 4, True, *step0)
    closure(own, (n_tiles // 2 - own) // 2, 2, False, *step0)
    kappa0 = kappas(0, total - 1)
    ce0, cn0 = coefficients(kappa0, low - 2, high + 2)
    de0, dn0 = diffs(c0, low - 2, high + 2)
    c1 = diffuse(c0, ce0, cn0, de0, dn0, low - 2, high + 2)
    for i in range(low - 2, high + 3):
        c_tiles1[tile_of[i]] = c1[i][0]
    c_tiles1[side_tile] = pack({i: c1[i][1] for i in range(low - 2, high + 3)})
    tiles1 = rows + 5
    for tile in range(tiles1, n_tiles):
        c_tiles1[tile] = zero
    step1 = (c_tiles1, slope1, x1, h1b1, h1f1, h2f1)
    closure(0, own // 4, 4, True, *step1)
    closure(own, 1, 2, True, *step1)
    closure(own + 2, 1, 1, False, *step1)
    kappa1 = kappas(low - 2, high + 2)
    ce1, cn1 = coefficients(kappa1, low - 1, high + 1)
    de1, dn1 = diffs(c1, low - 1, high + 1)
    c2 = diffuse(c1, ce1, cn1, de1, dn1, low, high)
    for i in range(low, high + 1):
        out_tracer[pl.ds(i - low, 8, stride=rows), :] = c2[i][0]
    lam2 = {}
    for i in range(low - 2, high + 3):
        lam2[i] = (tile_at(i, 1), unpack(side_l_packed, i))
    le, ln = diffs(lam2, low - 1, high + 1)
    direct = diffuse(lam2, ce1, cn1, le, ln, low - 1, high + 1)
    bars = kappa_bars(de1, dn1, le, ln, low - 1, high + 1)
    for i in range(low - 1, high + 2):
        d3_tiles[tile_of[i]] = bars[i][0]
    d3_tiles[side_tile] = pack({i: bars[i][1] for i in range(low, high + 1)})
    d3_tiles[rows + 3] = zero
    acc_w2[...] = jnp.zeros_like(acc_w2)
    acc_a1[...] = jnp.zeros_like(acc_a1)
    acc_head[...] = jnp.zeros_like(acc_head)
    closure_back(0, own // 4, 4, True, *step1[1:])
    closure_back(own, 1, 2, False, *step1[1:])
    side_bar = bar_tiles[side_tile]
    lam1 = {}
    for i in range(low - 1, high + 2):
        main = direct[i][0] + bar_tiles[tile_of[i]]
        side = direct[i][1] + unpack(side_bar, i)
        lam1[i] = (main, side)
    le, ln = diffs(lam1, low, high)
    direct = diffuse(lam1, ce0, cn0, le, ln, low, high)
    bars = kappa_bars(de0, dn0, le, ln, low, high)
    for i in range(low, high + 1):
        d3_tiles[tile_of[i]] = bars[i][0]
    closure_back(0, own // 4, 4, True, *step0[1:])
    for i in range(low, high + 1):
        out_grad[pl.ds(i - low, 8, stride=rows), :] = direct[i][0] + bar_tiles[tile_of[i]]
    first = [None] * 6

    def add(f, value):
        first[f] = value if first[f] is None else first[f] + value

    for k in range(DEPTH):
        cells = acc_a1[2 * HID * k : 2 * HID * k + HID, :]
        cells = cells + acc_a1[2 * HID * k + HID : 2 * HID * (k + 1), :]
        cells = jnp.concatenate([cells, jnp.zeros((HID, LANES - 32), F32)], 1)
        turned = jnp.transpose(cells)
        turned = turned[0:16] + turned[16:32]
        for t in range(2):
            add(t, turned[t * 4 + k : t * 4 + k + 1])
            if k >= 1:
                add(2 + t, -turned[8 + t * 4 + k - 1 : 8 + t * 4 + k])
            add(4 + t, turned[8 + t * 4 + k : 8 + t * 4 + k + 1])
    head = jnp.sum(jnp.transpose(acc_head[:, :LANES] + acc_head[:, LANES:]), 0, keepdims=True)
    rest = jnp.concatenate(first + [head, jnp.zeros_like(head)], 0)
    second = (acc_w2[:HID, :HID] + acc_w2[HID:, HID:]) + (acc_w2[:HID, HID:] + acc_w2[HID:, :HID])
    odd = jnp.bitwise_and(lax.axis_index("lat"), 1) == 1
    left, right = second[: HID // 2], second[HID // 2 :]
    out_keep[0 : HID // 2, :] = jnp.where(odd, right, left)
    out_give[0 : HID // 2, :] = jnp.where(odd, left, right)
    out_keep[HID // 2 :, :] = jnp.where(odd, 0.0, rest)
    out_give[HID // 2 :, :] = jnp.where(odd, rest, 0.0)


def finish_kernel(scale, mine, other, w1_out, w2_out, wh_out):
    odd = jnp.bitwise_and(lax.axis_index("lat"), 1) == 1
    half = HID // 2
    a, b = mine[...], other[...]
    left, right = jnp.where(odd, b, a) * scale, jnp.where(odd, a, b) * scale
    w2_out[0:half, :] = left[:half]
    w2_out[half:, :] = right[:half]
    w1_out[...] = left[half : half + 6]
    wh_out[...] = left[half + 6 : half + 7]


VMEM = pl.BlockSpec(memory_space=pltpu.VMEM)
SMEM = pl.BlockSpec(memory_space=pltpu.SMEM)
HBM = pl.BlockSpec(memory_space=pltpu.HBM)


def call(kernel, outs, ins, out_specs=None, scratch=(), limit=4 * 1024 * 1024, flops=1_000_000, size=1_000_000):
    return pl.pallas_call(
        kernel,
        out_shape=outs,
        in_specs=ins,
        out_specs=out_specs or [VMEM] * len(outs),
        scratch_shapes=list(scratch),
        compiler_params=pltpu.CompilerParams(vmem_limit_bytes=limit),
        cost_estimate=pl.CostEstimate(flops=flops, bytes_accessed=size, transcendentals=0),
    )


def shape(*dims, dtype=F32):
    return jax.ShapeDtypeStruct(dims, dtype)


def per_device(
    tracers,
    land_mask,
    level_counts,
    fold_partner,
    cotangent,
    w_first,
    b_first,
    w_second,
    b_second,
    w_head,
    b_head,
):
    rows, cols = land_mask.shape
    n_lon, n_lat = lax.axis_size("lon"), lax.axis_size("lat")
    tracer2 = tracers.reshape(8 * rows, cols)
    cot2 = cotangent.reshape(8 * rows, cols)

    args = (tracer2, cot2, land_mask, level_counts, fold_partner)
    south_first, north, south_last, turn = call(
        functools.partial(edges_kernel, rows, cols),
        [shape(48, LANES)] * 3 + [shape(1, dtype=jnp.int32)],
        [HBM] * len(args),
        out_specs=[VMEM] * 3 + [SMEM],
        scratch=[pltpu.VMEM(x.shape, x.dtype) for x in args[:4]]
        + [pltpu.SMEM(fold_partner.shape, fold_partner.dtype)]
        + [pltpu.SemaphoreType.DMA((len(args),))],
        limit=None,
    )(*args)

    def exchange(j, first, second, third):
        top = n_lat - 1

        def send(x, plain, fold):
            pairs = [
                (b * n_lat + source, b * n_lat + target)
                for b in range(n_lon)
                for source, target in plain
            ]
            if fold is not None:
                pairs += [
                    (b * n_lat + top, ((fold - b) % n_lon) * n_lat + top) for b in range(n_lon)
                ]
            return lax.ppermute(x, ("lon", "lat"), pairs)

        south = [(i + 1, i) for i in range(top - 1)] + [(0, top - 1)]
        north = [(i, i + 1) for i in range(top - 1)] + [(top - 1, 0)]
        last = [(i, i ^ 1) for i in range(n_lat)]
        return send(first, south, j), send(second, north, j - 1), send(third, last, None)

    from_first, from_second, from_third = lax.switch(
        turn[0],
        [functools.partial(exchange, j) for j in range(n_lon)],
        south_first,
        north,
        south_last,
    )

    total = rows + 2 * HALO
    ext, packed = call(
        functools.partial(assemble_kernel, rows),
        [shape(24 * total, LANES), shape(24, LANES)],
        [VMEM] * 8,
    )(
        fold_partner.reshape(1, cols),
        from_first,
        from_second,
        from_third,
        tracer2,
        cot2,
        land_mask,
        level_counts,
    )
    a1, w2t, w2, cols_w = call(
        weights_kernel,
        [
            shape(DEPTH * HID, 64, dtype=BF16),
            shape(2 * HID, 2 * HID, dtype=BF16),
            shape(2 * HID, 2 * HID, dtype=BF16),
            shape(8 * HID + 8, LANES),
        ],
        [VMEM] * 6,
    )(
        w_first,
        b_first.reshape(1, HID),
        w_second,
        b_second.reshape(1, HID),
        w_head.reshape(1, HID),
        b_head.reshape(1, 1),
    )
    from_west = lax.ppermute(packed, "lon", [(i, (i + 1) % n_lon) for i in range(n_lon)])
    from_east = lax.ppermute(packed, "lon", [((i + 1) % n_lon, i) for i in range(n_lon)])

    n_tiles = total + 1 + (total + 1) % 2
    pairs0 = rows // 2
    pairs1 = rows // 2 + 2
    tiles = pltpu.VMEM((n_tiles, 8, LANES), F32)
    wide = 2 * LANES
    scratch = (
        [tiles] * 9
        + [pltpu.VMEM((n, 64, wide), BF16) for n in (pairs0, pairs1)]
        + [pltpu.VMEM((n, DEPTH, 2 * HID, wide), BF16) for n in (pairs0, pairs1)]
        + [pltpu.VMEM((n, DEPTH, HID, wide), F32) for n in (pairs0, pairs1)]
        + [pltpu.VMEM((n, DEPTH, HID, wide), F32) for n in (pairs0, pairs1)]
        + [
            pltpu.VMEM((2 * HID, 2 * HID), F32),
            pltpu.VMEM((DEPTH * 2 * HID, 32), F32),
            pltpu.VMEM((HID, wide), F32),
        ]
    )
    final, grad, keep, give = call(
        functools.partial(steps_kernel, rows),
        [shape(8 * rows, LANES)] * 2 + [shape(HID // 2 + 8, LANES)] * 2,
        [VMEM] * 7,
        scratch=scratch,
        limit=36 * 1024 * 1024,
        flops=10_000_000_000,
    )(ext, from_west, from_east, a1, w2t, w2, cols_w)

    def swap(x, mask):
        pairs = [(i, i ^ mask) for i in range(n_lon * n_lat)]
        return lax.ppermute(x, ("lon", "lat"), pairs)

    sums = keep + swap(give, 1)
    bits = [1 << b for b in range(1, (n_lon * n_lat).bit_length() - 1)]
    while bits:
        a, bits = bits[0], bits[1:]
        if bits:
            b, bits = bits[0], bits[1:]
            near, far, both = swap(sums, a), swap(sums, b), swap(sums, a | b)
            sums = (sums + near) + (far + both)
        else:
            sums = sums + swap(sums, a)
    other = swap(sums, 1)
    scale = 1.0 / math.sqrt(n_lon * cols * n_lat * rows * DEPTH)
    first_grad, second_grad, head_grad = call(
        functools.partial(finish_kernel, scale),
        [shape(6, HID), shape(HID, HID), shape(1, HID)],
        [VMEM] * 2,
    )(sums, other)
    return (
        final.reshape(tracers.shape),
        grad.reshape(tracers.shape),
        first_grad,
        second_grad,
        head_grad.reshape(HID),
    )


def solution(mesh):
    return jax.shard_map(
        per_device,
        mesh=mesh,
        in_specs=(
            P(None, None, "lat", "lon"),
            P("lat", "lon"),
            P("lat", "lon"),
            P("lon"),
            P(None, None, "lat", "lon"),
            P(),
            P(),
            P(),
            P(),
            P(),
            P(),
        ),
        out_specs=(P(None, None, "lat", "lon"), P(None, None, "lat", "lon"), P(), P(), P()),
        check_vma=False,
    )
```

```python
import functools
import math

import jax
import jax.numpy as jnp
from jax import lax
from jax.experimental import pallas as pl
from jax.experimental.pallas import tpu as pltpu
from jax.sharding import PartitionSpec as P

KMAX = 0.24
DEPTH = 4
HID = 128
LANES = 128
HALO = 3
GROUP = 8
SLOT = 2 * HALO
F32 = jnp.float32
BF16 = jnp.bfloat16


def split(x):
    high = x.astype(BF16)
    low = (x - high.astype(F32)).astype(BF16)
    return high, low


def iota(shape, dim):
    return lax.broadcasted_iota(jnp.int32, shape, dim)


def edges_kernel(
    rows,
    cols,
    tracer_hbm,
    cot_hbm,
    land_hbm,
    levels_hbm,
    partner_hbm,
    south_first,
    north,
    south_last,
    turn_out,
    source_out,
    tracer,
    cot,
    land,
    levels,
    partner,
    sems,
):
    pairs = (
        (partner_hbm, partner),
        (tracer_hbm, tracer),
        (cot_hbm, cot),
        (land_hbm, land),
        (levels_hbm, levels),
    )
    copies = [
        pltpu.make_async_copy(source, target, sems.at[n])
        for n, (source, target) in enumerate(pairs)
    ]
    for copy in copies:
        copy.start()
    for copy in copies:
        copy.wait()
    turn_out[0] = lax.rem(lax.div(partner[0], cols) + lax.axis_index("lon"), lax.axis_size("lon"))

    lane = iota((8, LANES), 1)
    source_out[...] = jnp.bitwise_and(partner[0] - lane, LANES - 1)

    at_top = lax.axis_index("lat") == lax.axis_size("lat") - 1
    depth = (land[...] * levels[...]).astype(F32)

    def edge(first, skip):
        parts = [tracer[pl.ds(first + j, 8, stride=rows), :] for j in range(HALO)]
        parts += [cot[pl.ds(first + skip + j, 8, stride=rows), :] for j in range(2)]
        parts += [depth[first : first + HALO], jnp.zeros((8 - HALO, LANES), F32)]
        return jnp.concatenate(parts, 0)

    low, high = edge(0, 0), edge(rows - HALO, 1)
    south_first[...] = jnp.where(at_top, high, low)
    north[...] = high
    south_last[...] = jnp.where(at_top, low, high)


def weights_kernel(w1, b1, w2, b2, wh, bh, a1_out, w2t_out, w2_out, col_out):
    first = w1[...]
    bias_high, bias_low = split(b1[...])
    row = iota((16, LANES), 0)
    pad_row = iota((16, LANES), 0)
    for k in range(DEPTH):
        block = jnp.zeros((16, LANES), F32)
        for t in range(2):
            block = jnp.where(row == t * 4 + k, first[t : t + 1], block)
            if k >= 1:
                block = jnp.where(row == 8 + t * 4 + k - 1, -first[2 + t : 3 + t], block)
            block = jnp.where(row == 8 + t * 4 + k, first[4 + t : 5 + t], block)
        high, low = split(block)
        high32, low32 = high.astype(F32), low.astype(F32)
        tail = jnp.where(
            pad_row == 0,
            bias_high.astype(F32),
            jnp.where(pad_row == 1, bias_low.astype(F32), 0.0),
        )
        tall = jnp.concatenate([high32, high32, low32, tail, jnp.zeros((64, LANES), F32)], 0)
        a1_out[k * HID : (k + 1) * HID, :] = jnp.transpose(tall)[:, :64].astype(BF16)
    second = w2[...]
    for out, matrix in ((w2_out, second), (w2t_out, jnp.transpose(second))):
        high, low = split(matrix)
        out[0:HID, :] = jnp.concatenate([high, high], 1)
        out[HID : 2 * HID, :] = jnp.concatenate([low, low], 1)
    vectors = [b2[...], wh[...]] + [first[f : f + 1] for f in range(6)]
    for n, vector in enumerate(vectors):
        column = jnp.transpose(jnp.broadcast_to(vector, (HID, LANES)))
        col_out[n * HID : (n + 1) * HID, :] = column
    col_out[8 * HID : 8 * HID + 8, :] = jnp.broadcast_to(bh[...], (8, LANES))


def assemble_kernel(
    rows, source_in, first, second, third, tracer, cot, land, levels, ext, packed
):
    lane = iota((8, LANES), 1)
    lat, n_lat = lax.axis_index("lat"), lax.axis_size("lat")
    at_top = lat == n_lat - 1
    below_top = lat == n_lat - 2
    at_bottom = lat == 0
    source = source_in[...]
    offset = jnp.broadcast_to(source[:, 0:1], (8, LANES))

    def mirrored(place):
        both = jnp.where(
            lane <= offset, first[place : place + 8, :], second[place : place + 8, :]
        )
        return jnp.take_along_axis(both, source, axis=1)

    zero = jnp.zeros((8, LANES), F32)

    def from_north(place):
        return jnp.where(below_top, third[place : place + 8, :], first[place : place + 8, :])

    def from_south(place):
        near = jnp.where(at_top, third[place : place + 8, :], second[place : place + 8, :])
        return jnp.where(at_bottom, 0.0, near)

    def north(plain, folded):
        return jnp.where(at_top, mirrored(folded), from_north(plain))

    def spread(tile, j):
        return jnp.broadcast_to(tile[j : j + 1], (8, LANES))

    depth_here = (land[...] * levels[...]).astype(F32)
    depth_south = from_south(40)
    depth_north = from_north(40)
    depth_fold = mirrored(40)
    total = rows + 2 * HALO
    tiles = []
    for i in range(total):
        r = i - HALO
        if r < 0:
            tile_c = from_south(8 * i)
            tile_l = from_south(24 + 8 * (i - 1)) if i >= 1 else zero
            tile_n = spread(depth_south, i)
        elif r < rows:
            tile_c = tracer[pl.ds(r, 8, stride=rows), :]
            tile_l = cot[pl.ds(r, 8, stride=rows), :]
            tile_n = spread(depth_here, r)
        else:
            j = r - rows
            tile_c = north(8 * j, 8 * (2 - j))
            tile_l = north(24 + 8 * j, 24 + 8 * (1 - j)) if j < 2 else zero
            tile_n = jnp.where(at_top, spread(depth_fold, 2 - j), spread(depth_north, j))
        tiles.append((tile_c, tile_l, tile_n))
        for part, tile in enumerate(tiles[-1]):
            ext[24 * i + 8 * part : 24 * i + 8 * part + 8, :] = tile
    for part in range(3):
        acc = zero
        for slot in range(rows + 4):
            moved = pltpu.roll(tiles[slot + 1][part], SLOT * slot + HALO, 1)
            inside = (lane >= SLOT * slot) & (lane < SLOT * slot + SLOT)
            acc = jnp.where(inside, moved, acc)
        packed[8 * part : 8 * part + 8, :] = acc


def steps_kernel(
    rows,
    ext,
    west_in,
    east_in,
    a1,
    w2t,
    w2,
    cols,
    out_tracer,
    out_grad,
    out_keep,
    out_give,
    c_tiles0,
    c_tiles1,
    wv_tiles,
    wet_tiles,
    kappa_tiles,
    slope0,
    slope1,
    d3_tiles,
    bar_tiles,
    x0,
    x1,
    h1b0,
    h1b1,
    h1f0,
    h1f1,
    h2f0,
    h2f1,
    acc_w2,
    acc_a1,
    acc_head,
):
    total = rows + 2 * HALO
    lane = iota((8, LANES), 1)
    level = jnp.bitwise_and(iota((8, LANES), 0), DEPTH - 1)
    level_wide = jnp.bitwise_and(iota((8, 2 * LANES), 0), DEPTH - 1)
    zero = jnp.zeros((8, LANES), F32)
    side_tile = rows
    tile_of = {i: i - HALO for i in range(HALO, rows + HALO)}
    place = rows + 1
    for ring in (1, 2, 3):
        tile_of[HALO - ring] = place
        tile_of[rows + HALO - 1 + ring] = place + 1
        place += 2
    n_tiles = place + (place % 2)
    slots = range(1, rows + 5)

    def east(main, side):
        return (
            pltpu.roll(jnp.where(lane == 0, side, main), LANES - 1, 1),
            pltpu.roll(jnp.where(lane == 0, main, side), LANES - 1, 1),
        )

    def from_west(main, side):
        return (
            pltpu.roll(jnp.where(lane == LANES - 1, side, main), 1, 1),
            pltpu.roll(jnp.where(lane == LANES - 1, main, side), 1, 1),
        )

    def from_west_main(main, side):
        return pltpu.roll(jnp.where(lane == LANES - 1, side, main), 1, 1)

    def unpack(tile, i):
        return pltpu.roll(tile, LANES - (SLOT * (i - 1) + HALO), 1)

    def pack(tiles):
        acc = zero
        for i, tile in tiles.items():
            slot = i - 1
            moved = pltpu.roll(tile, SLOT * slot + HALO, 1)
            inside = (lane >= SLOT * slot) & (lane < SLOT * slot + SLOT)
            acc = jnp.where(inside, moved, acc)
        return acc

    def column(n):
        part = cols[n * HID : (n + 1) * HID, :]
        return jnp.concatenate([part, part], 1)

    head_bias = cols[8 * HID : 8 * HID + 1, :][:, 0:1]

    def both(x):
        return x + pltpu.roll(x, 4, 0)

    third = lax.rem(lane, SLOT)
    from_left = third < HALO
    side_c_packed = jnp.where(from_left, west_in[0:8, :], east_in[0:8, :])
    side_l_packed = jnp.where(from_left, west_in[8:16, :], east_in[8:16, :])
    side_n_packed = jnp.where(from_left, west_in[16:24, :], east_in[16:24, :])
    side_lanes = (lane < HALO) | (lane >= LANES - HALO)

    def wet_of(depth):
        return jnp.where(depth > level.astype(F32), 1.0, 0.0)

    def vertical_of(depth):
        inside = (depth > (level + 1).astype(F32)) & (level < DEPTH - 1)
        return jnp.where(inside, 1.0, 0.0)

    def tile_at(i, part):
        place = 24 * i + 8 * part
        return ext[place : place + 8, :]

    c0, wet = {}, {}
    for i in range(total):
        depth = tile_at(i, 2)
        main_c = tile_at(i, 0)
        main_w = wet_of(depth)
        if i in slots:
            side_c = unpack(side_c_packed, i)
            side_w = jnp.where(side_lanes, wet_of(unpack(side_n_packed, i)), 0.0)
        else:
            side_c, side_w = zero, zero
        c0[i] = (main_c, side_c)
        wet[i] = (main_w, side_w)
        c_tiles0[tile_of[i]] = main_c
        wet_tiles[tile_of[i]] = main_w
        wv_tiles[tile_of[i]] = vertical_of(depth)
    c_tiles0[side_tile] = side_c_packed
    wet_tiles[side_tile] = wet_of(side_n_packed)
    wv_tiles[side_tile] = vertical_of(side_n_packed)
    for tile in range(place, n_tiles):
        c_tiles0[tile] = zero
        wet_tiles[tile] = zero
        wv_tiles[tile] = zero

    def closure(start, steps, group, save, c_tiles, slope, xs, h1b, h1f, h2f):
        def body(step, carry):
            first_pair = start + step * group
            items = [(first_pair + g, k) for g in range(group) for k in range(DEPTH)]
            inputs = []
            for g in range(group):
                p = first_pair + g
                pieces = []
                for a in range(2):
                    c = c_tiles[2 * p + a]
                    v = (pltpu.roll(c, 7, 0) - c) * wv_tiles[2 * p + a]
                    pieces.append(jnp.concatenate([c, v], 0))
                high, low = split(jnp.concatenate(pieces, 1))
                x = jnp.concatenate([high, low, high, jnp.ones((16, 2 * LANES), BF16)], 0)
                if save:
                    xs[p] = x
                inputs.append(jnp.dot(a1[...], x, preferred_element_type=F32))
            outs = [jnp.zeros((8, 2 * LANES), F32)] * group
            pairs = {}
            for j in range(len(items) + 1):
                if j < len(items):
                    p, k = items[j]
                    h1 = jnp.tanh(inputs[j // DEPTH][k * HID : (k + 1) * HID])
                    pairs[j] = jnp.concatenate(split(h1), 0)
                    if save:
                        h1f[p, k] = h1
                        h1b[p, k] = pairs[j]
                if j >= 1:
                    p, k = items[j - 1]
                    z = jnp.dot(w2t[...], pairs.pop(j - 1), preferred_element_type=F32)
                    h2 = jnp.tanh(z[:HID] + z[HID:] + column(0))
                    if save:
                        h2f[p, k] = h2
                    head = jnp.sum(h2 * column(1), 0, keepdims=True)
                    g = (j - 1) // DEPTH
                    outs[g] = jnp.where(level_wide == k, head, outs[g])
            for g in range(group):
                sig = jax.nn.sigmoid(outs[g] + head_bias)
                for a in range(2):
                    tile = 2 * (first_pair + g) + a
                    part = sig[:, a * LANES : (a + 1) * LANES]
                    kappa = KMAX * part * wet_tiles[tile]
                    kappa_tiles[tile] = kappa
                    slope[tile] = kappa * (1.0 - part)
            return carry

        if steps == 1:
            body(0, 0)
        else:
            lax.fori_loop(0, steps, body, 0)

    def edge_masks(i):
        east_w = east(*wet[i])
        return tuple(0.5 * a * b for a, b in zip(wet[i], east_w))

    def north_mask(i):
        return tuple(0.5 * a * b for a, b in zip(wet[i], wet[i + 1]))

    def kappas(lo, hi):
        packed = kappa_tiles[side_tile]
        out = {}
        for i in range(lo, hi + 1):
            side = unpack(packed, i) if i in slots else zero
            out[i] = (kappa_tiles[tile_of[i]], side)
        return out

    def coefficients(kappa, lo, hi):
        ce, cn = {}, {}
        for i in range(lo, hi + 1):
            ke = east(*kappa[i])
            ce[i] = tuple(m * (a + b) for m, a, b in zip(edge_masks(i), kappa[i], ke))
        for i in range(lo - 1, hi + 1):
            cn[i] = tuple(
                m * (a + b) for m, a, b in zip(north_mask(i), kappa[i], kappa[i + 1])
            )
        return ce, cn

    def diffs(field, lo, hi):
        de, dn = {}, {}
        for i in range(lo, hi + 1):
            fe = east(*field[i])
            de[i] = tuple(b - a for a, b in zip(field[i], fe))
        for i in range(lo - 1, hi + 1):
            dn[i] = tuple(b - a for a, b in zip(field[i], field[i + 1]))
        return de, dn

    def diffuse(field, ce, cn, de, dn, lo, hi):
        out = {}
        flux_n = {i: tuple(c * d for c, d in zip(cn[i], dn[i])) for i in range(lo - 1, hi + 1)}
        for i in range(lo, hi + 1):
            fe = tuple(c * d for c, d in zip(ce[i], de[i]))
            fw = from_west(*fe)
            out[i] = tuple(
                f + ((a - b) + (c - d))
                for f, a, b, c, d in zip(field[i], fe, fw, flux_n[i], flux_n[i - 1])
            )
        return out

    def kappa_bars(de, dn, le, ln, lo, hi):
        out = {}
        gn = {}
        for i in range(lo - 1, hi + 1):
            gn[i] = tuple(-m * a * b for m, a, b in zip(north_mask(i), dn[i], ln[i]))
        for i in range(lo, hi + 1):
            ge = tuple(-m * a * b for m, a, b in zip(edge_masks(i), de[i], le[i]))
            gw = from_west(*ge)
            out[i] = tuple(
                both((a + b) + (c + d)) for a, b, c, d in zip(ge, gw, gn[i], gn[i - 1])
            )
        return out

    def outer(left, right):
        return lax.dot_general(
            left, right, (((1,), (1,)), ((), ())), preferred_element_type=F32
        )

    sublane_wide = iota((8, 2 * LANES), 0)

    def groups(x):
        return jnp.sum(x.reshape(HID // 8, 8, 2 * LANES), 0)

    def put_row(bars, n, row, part):
        value = jnp.where(sublane_wide == row, jnp.sum(part, 0, keepdims=True), 0.0)
        bars = list(bars)
        bars[n] = plus(bars[n], value)
        return bars

    def plus(left, right):
        return right if left is None else left + right

    def closure_back(start, steps, group, with_sums, slope, xs, h1b, h1f, h2f):
        def body(step, carry):
            first_pair = start + step * group
            items = [(first_pair + g, k) for g in range(group) for k in range(DEPTH)]
            d3 = [
                jnp.concatenate(
                    [
                        d3_tiles[2 * (first_pair + g) + a] * slope[2 * (first_pair + g) + a]
                        for a in range(2)
                    ],
                    1,
                )
                for g in range(group)
            ]
            bars = [[None] * 6 for g in range(group)]
            sum_w2, sum_head, sum_a1 = None, None, None
            seconds, firsts = {}, {}
            for j in range(len(items) + 2):
                if j < len(items):
                    p, k = items[j]
                    h2 = h2f[p, k]
                    row = d3[j // DEPTH][k : k + 1]
                    d2 = (column(1) * row) * (1.0 - h2 * h2)
                    seconds[j] = jnp.concatenate(split(d2), 0)
                    if with_sums:
                        sum_head = plus(sum_head, h2 * row)
                if 1 <= j <= len(items):
                    p, k = items[j - 1]
                    d2b = seconds.pop(j - 1)
                    e = jnp.dot(w2[...], d2b, preferred_element_type=F32)
                    h1 = h1f[p, k]
                    d1 = (e[:HID] + e[HID:]) * (1.0 - h1 * h1)
                    firsts[j - 1] = d1
                    if with_sums:
                        sum_w2 = plus(sum_w2, outer(h1b[p, k], d2b))
                if j >= 2:
                    p, k = items[j - 2]
                    g = (j - 2) // DEPTH
                    d1 = firsts.pop(j - 2)
                    if with_sums:
                        seconds[g, k] = jnp.concatenate(split(d1), 0)
                        if k == DEPTH - 1:
                            d1b = jnp.concatenate([seconds.pop((g, n)) for n in range(DEPTH)], 0)
                            sum_a1 = plus(sum_a1, outer(d1b, xs[p, 0:32, :]))
                    parts = [groups(d1 * column(2 + f)) for f in range(6)]
                    for t in range(2):
                        bars[g] = put_row(bars[g], t, t * DEPTH + k, parts[t])
                        if k >= 1:
                            below = bars[g][2 + t]
                            bars[g] = put_row(
                                bars[g], 4 + t, t * DEPTH + k - 1, below - parts[2 + t]
                            )
                        bars[g][2 + t] = parts[4 + t]
            if with_sums:
                acc_w2[...] += sum_w2
                acc_head[...] += sum_head
                acc_a1[...] += sum_a1
            for g in range(group):
                cells = plus(bars[g][0], bars[g][1])
                vertical = plus(bars[g][4], bars[g][5])
                for a in range(2):
                    tile = 2 * (first_pair + g) + a
                    lanes = slice(a * LANES, (a + 1) * LANES)
                    v = vertical[:, lanes] * wv_tiles[tile]
                    bar_tiles[tile] = cells[:, lanes] - v + pltpu.roll(v, 1, 0)
            return carry

        if steps == 1:
            body(0, 0)
        else:
            lax.fori_loop(0, steps, body, 0)

    low, high = HALO, rows + HALO - 1
    step0 = (c_tiles0, slope0, x0, h1b0, h1f0, h2f0)
    own = rows // 2
    closure(0, own // GROUP, GROUP, True, *step0)
    closure(own, 1, n_tiles // 2 - own, False, *step0)
    kappa0 = kappas(0, total - 1)
    ce0, cn0 = coefficients(kappa0, low - 2, high + 2)
    de0, dn0 = diffs(c0, low - 2, high + 2)
    c1 = diffuse(c0, ce0, cn0, de0, dn0, low - 2, high + 2)
    for i in range(low - 2, high + 3):
        c_tiles1[tile_of[i]] = c1[i][0]
    c_tiles1[side_tile] = pack({i: c1[i][1] for i in range(low - 2, high + 3)})
    tiles1 = rows + 5
    for tile in range(tiles1, n_tiles):
        c_tiles1[tile] = zero
    step1 = (c_tiles1, slope1, x1, h1b1, h1f1, h2f1)
    closure(0, own // GROUP, GROUP, True, *step1)
    closure(own, 1, 2, True, *step1)
    closure(own + 2, 1, 1, False, *step1)
    kappa1 = kappas(low - 2, high + 2)
    ce1, cn1 = coefficients(kappa1, low - 1, high + 1)
    de1, dn1 = diffs(c1, low - 1, high + 1)
    c2 = diffuse(c1, ce1, cn1, de1, dn1, low, high)
    for i in range(low, high + 1):
        out_tracer[pl.ds(i - low, 8, stride=rows), :] = c2[i][0]
    lam2 = {}
    for i in range(low - 2, high + 3):
        lam2[i] = (tile_at(i, 1), unpack(side_l_packed, i))
    le, ln = diffs(lam2, low - 1, high + 1)
    direct = diffuse(lam2, ce1, cn1, le, ln, low - 1, high + 1)
    bars = kappa_bars(de1, dn1, le, ln, low - 1, high + 1)
    for i in range(low - 1, high + 2):
        d3_tiles[tile_of[i]] = bars[i][0]
    d3_tiles[side_tile] = pack({i: bars[i][1] for i in range(low, high + 1)})
    d3_tiles[rows + 3] = zero
    acc_w2[...] = jnp.zeros_like(acc_w2)
    acc_a1[...] = jnp.zeros_like(acc_a1)
    acc_head[...] = jnp.zeros_like(acc_head)
    closure_back(0, own // GROUP, GROUP, True, *step1[1:])
    closure_back(own, 1, 2, False, *step1[1:])
    side_bar = bar_tiles[side_tile]
    lam1 = {}
    for i in range(low - 1, high + 2):
        main = direct[i][0] + bar_tiles[tile_of[i]]
        side = direct[i][1] + unpack(side_bar, i)
        lam1[i] = (main, side)
    le, ln = diffs(lam1, low, high)
    direct = diffuse(lam1, ce0, cn0, le, ln, low, high)
    bars = kappa_bars(de0, dn0, le, ln, low, high)
    for i in range(low, high + 1):
        d3_tiles[tile_of[i]] = bars[i][0]
    closure_back(0, own // GROUP, GROUP, True, *step0[1:])
    for i in range(low, high + 1):
        out_grad[pl.ds(i - low, 8, stride=rows), :] = direct[i][0] + bar_tiles[tile_of[i]]
    first = [None] * 6

    def add(f, value):
        first[f] = value if first[f] is None else first[f] + value

    for k in range(DEPTH):
        cells = acc_a1[2 * HID * k : 2 * HID * k + HID, :]
        cells = cells + acc_a1[2 * HID * k + HID : 2 * HID * (k + 1), :]
        cells = jnp.concatenate([cells, jnp.zeros((HID, LANES - 32), F32)], 1)
        turned = jnp.transpose(cells)
        turned = turned[0:16] + turned[16:32]
        for t in range(2):
            add(t, turned[t * 4 + k : t * 4 + k + 1])
            if k >= 1:
                add(2 + t, -turned[8 + t * 4 + k - 1 : 8 + t * 4 + k])
            add(4 + t, turned[8 + t * 4 + k : 8 + t * 4 + k + 1])
    head = jnp.sum(jnp.transpose(acc_head[:, :LANES] + acc_head[:, LANES:]), 0, keepdims=True)
    rest = jnp.concatenate(first + [head, jnp.zeros_like(head)], 0)
    second = (acc_w2[:HID, :HID] + acc_w2[HID:, HID:]) + (acc_w2[:HID, HID:] + acc_w2[HID:, :HID])
    odd = jnp.bitwise_and(lax.axis_index("lat"), 1) == 1
    left, right = second[: HID // 2], second[HID // 2 :]
    out_keep[0 : HID // 2, :] = jnp.where(odd, right, left)
    out_give[0 : HID // 2, :] = jnp.where(odd, left, right)
    out_keep[HID // 2 :, :] = jnp.where(odd, 0.0, rest)
    out_give[HID // 2 :, :] = jnp.where(odd, rest, 0.0)


def finish_kernel(scale, mine, other, w1_out, w2_out, wh_out):
    odd = jnp.bitwise_and(lax.axis_index("lat"), 1) == 1
    half = HID // 2
    a, b = mine[...], other[...]
    left, right = jnp.where(odd, b, a) * scale, jnp.where(odd, a, b) * scale
    w2_out[0:half, :] = left[:half]
    w2_out[half:, :] = right[:half]
    w1_out[...] = left[half : half + 6]
    wh_out[...] = left[half + 6 : half + 7]


VMEM = pl.BlockSpec(memory_space=pltpu.VMEM)
SMEM = pl.BlockSpec(memory_space=pltpu.SMEM)
HBM = pl.BlockSpec(memory_space=pltpu.HBM)


def call(kernel, outs, ins, out_specs=None, scratch=(), limit=4 * 1024 * 1024, flops=1_000_000, size=1_000_000):
    return pl.pallas_call(
        kernel,
        out_shape=outs,
        in_specs=ins,
        out_specs=out_specs or [VMEM] * len(outs),
        scratch_shapes=list(scratch),
        compiler_params=pltpu.CompilerParams(vmem_limit_bytes=limit),
        cost_estimate=pl.CostEstimate(flops=flops, bytes_accessed=size, transcendentals=0),
    )


def shape(*dims, dtype=F32):
    return jax.ShapeDtypeStruct(dims, dtype)


def per_device(
    tracers,
    land_mask,
    level_counts,
    fold_partner,
    cotangent,
    w_first,
    b_first,
    w_second,
    b_second,
    w_head,
    b_head,
):
    rows, cols = land_mask.shape
    n_lon, n_lat = lax.axis_size("lon"), lax.axis_size("lat")
    tracer2 = tracers.reshape(8 * rows, cols)
    cot2 = cotangent.reshape(8 * rows, cols)

    args = (tracer2, cot2, land_mask, level_counts, fold_partner)
    south_first, north, south_last, turn, source = call(
        functools.partial(edges_kernel, rows, cols),
        [shape(48, LANES)] * 3 + [shape(1, dtype=jnp.int32), shape(8, LANES, dtype=jnp.int32)],
        [HBM] * len(args),
        out_specs=[VMEM] * 3 + [SMEM, VMEM],
        scratch=[pltpu.VMEM(x.shape, x.dtype) for x in args[:4]]
        + [pltpu.SMEM(fold_partner.shape, fold_partner.dtype)]
        + [pltpu.SemaphoreType.DMA((len(args),))],
        limit=None,
    )(*args)

    def exchange(j, first, second, third):
        top = n_lat - 1

        def send(x, plain, fold):
            pairs = [
                (b * n_lat + source, b * n_lat + target)
                for b in range(n_lon)
                for source, target in plain
            ]
            if fold is not None:
                pairs += [
                    (b * n_lat + top, ((fold - b) % n_lon) * n_lat + top) for b in range(n_lon)
                ]
            return lax.ppermute(x, ("lon", "lat"), pairs)

        south = [(i + 1, i) for i in range(top - 1)] + [(0, top - 1)]
        north = [(i, i + 1) for i in range(top - 1)] + [(top - 1, 0)]
        last = [(i, i ^ 1) for i in range(n_lat)]
        return send(first, south, j), send(second, north, j - 1), send(third, last, None)

    from_first, from_second, from_third = lax.switch(
        turn[0],
        [functools.partial(exchange, j) for j in range(n_lon)],
        south_first,
        north,
        south_last,
    )

    total = rows + 2 * HALO
    ext, packed = call(
        functools.partial(assemble_kernel, rows),
        [shape(24 * total, LANES), shape(24, LANES)],
        [VMEM] * 8,
    )(
        source,
        from_first,
        from_second,
        from_third,
        tracer2,
        cot2,
        land_mask,
        level_counts,
    )
    a1, w2t, w2, cols_w = call(
        weights_kernel,
        [
            shape(DEPTH * HID, 64, dtype=BF16),
            shape(2 * HID, 2 * HID, dtype=BF16),
            shape(2 * HID, 2 * HID, dtype=BF16),
            shape(8 * HID + 8, LANES),
        ],
        [VMEM] * 6,
    )(
        w_first,
        b_first.reshape(1, HID),
        w_second,
        b_second.reshape(1, HID),
        w_head.reshape(1, HID),
        b_head.reshape(1, 1),
    )
    from_west = lax.ppermute(packed, "lon", [(i, (i + 1) % n_lon) for i in range(n_lon)])
    from_east = lax.ppermute(packed, "lon", [((i + 1) % n_lon, i) for i in range(n_lon)])

    n_tiles = total + 1 + (total + 1) % 2
    pairs0 = rows // 2
    pairs1 = rows // 2 + 2
    tiles = pltpu.VMEM((n_tiles, 8, LANES), F32)
    wide = 2 * LANES
    scratch = (
        [tiles] * 9
        + [pltpu.VMEM((n, 64, wide), BF16) for n in (pairs0, pairs1)]
        + [pltpu.VMEM((n, DEPTH, 2 * HID, wide), BF16) for n in (pairs0, pairs1)]
        + [pltpu.VMEM((n, DEPTH, HID, wide), F32) for n in (pairs0, pairs1)]
        + [pltpu.VMEM((n, DEPTH, HID, wide), F32) for n in (pairs0, pairs1)]
        + [
            pltpu.VMEM((2 * HID, 2 * HID), F32),
            pltpu.VMEM((DEPTH * 2 * HID, 32), F32),
            pltpu.VMEM((HID, wide), F32),
        ]
    )
    final, grad, keep, give = call(
        functools.partial(steps_kernel, rows),
        [shape(8 * rows, LANES)] * 2 + [shape(HID // 2 + 8, LANES)] * 2,
        [VMEM] * 7,
        scratch=scratch,
        limit=36 * 1024 * 1024,
        flops=10_000_000_000,
    )(ext, from_west, from_east, a1, w2t, w2, cols_w)

    def swap(x, mask):
        pairs = [(i, i ^ mask) for i in range(n_lon * n_lat)]
        return lax.ppermute(x, ("lon", "lat"), pairs)

    sums = keep + swap(give, 1)
    bits = [1 << b for b in range(1, (n_lon * n_lat).bit_length() - 1)]
    while bits:
        a, bits = bits[0], bits[1:]
        if bits:
            b, bits = bits[0], bits[1:]
            near, far, both = swap(sums, a), swap(sums, b), swap(sums, a | b)
            sums = (sums + near) + (far + both)
        else:
            sums = sums + swap(sums, a)
    other = swap(sums, 1)
    scale = 1.0 / math.sqrt(n_lon * cols * n_lat * rows * DEPTH)
    first_grad, second_grad, head_grad = call(
        functools.partial(finish_kernel, scale),
        [shape(6, HID), shape(HID, HID), shape(1, HID)],
        [VMEM] * 2,
    )(sums, other)
    return (
        final.reshape(tracers.shape),
        grad.reshape(tracers.shape),
        first_grad,
        second_grad,
        head_grad.reshape(HID),
    )


def solution(mesh):
    return jax.shard_map(
        per_device,
        mesh=mesh,
        in_specs=(
            P(None, None, "lat", "lon"),
            P("lat", "lon"),
            P("lat", "lon"),
            P("lon"),
            P(None, None, "lat", "lon"),
            P(),
            P(),
            P(),
            P(),
            P(),
            P(),
        ),
        out_specs=(P(None, None, "lat", "lon"), P(None, None, "lat", "lon"), P(), P(), P()),
        check_vma=False,
    )
```

```python
import functools
import math

import jax
import jax.numpy as jnp
from jax import lax
from jax.experimental import pallas as pl
from jax.experimental.pallas import tpu as pltpu
from jax.sharding import PartitionSpec as P

KMAX = 0.24
DEPTH = 4
HID = 128
LANES = 128
HALO = 3
GROUP = 8
SLOT = 2 * HALO
F32 = jnp.float32
BF16 = jnp.bfloat16


def split(x):
    high = x.astype(BF16)
    low = (x - high.astype(F32)).astype(BF16)
    return high, low


def iota(shape, dim):
    return lax.broadcasted_iota(jnp.int32, shape, dim)


def edges_kernel(
    rows,
    cols,
    tracer_hbm,
    cot_hbm,
    land_hbm,
    levels_hbm,
    partner_hbm,
    near_out,
    north_out,
    chip_out,
    turn_out,
    tracer,
    cot,
    land,
    levels,
    partner,
    sems,
):
    pairs = (
        (partner_hbm, partner),
        (tracer_hbm, tracer),
        (cot_hbm, cot),
        (land_hbm, land),
        (levels_hbm, levels),
    )
    copies = [
        pltpu.make_async_copy(source, target, sems.at[n])
        for n, (source, target) in enumerate(pairs)
    ]
    for copy in copies:
        copy.start()
    for copy in copies:
        copy.wait()
    turn_out[0] = lax.rem(lax.div(partner[0], cols) + lax.axis_index("lon"), lax.axis_size("lon"))

    facing = jnp.bitwise_and(partner[0] - iota((1, LANES), 1), LANES - 1).astype(F32)
    odd = lax.rem(lax.axis_index("lat"), 2) == 1
    depth = (land[...] * levels[...]).astype(F32)

    def edge(first, skip):
        parts = [tracer[pl.ds(first + j, 8, stride=rows), :] for j in range(HALO)]
        parts += [cot[pl.ds(first + skip + j, 8, stride=rows), :] for j in range(2)]
        parts += [depth[first : first + HALO], facing, jnp.zeros((7 - HALO, LANES), F32)]
        return jnp.concatenate(parts, 0)

    low, high = edge(0, 0), edge(rows - HALO, 1)
    near_out[...] = jnp.where(odd, high, low)
    north_out[...] = high
    chip_out[...] = jnp.where(odd, low, high)


def weights_kernel(w1, b1, w2, b2, wh, bh, a1_out, w2t_out, w2_out, col_out):
    first = w1[...]
    bias_high, bias_low = split(b1[...])
    row = iota((16, LANES), 0)
    pad_row = iota((16, LANES), 0)
    for k in range(DEPTH):
        block = jnp.zeros((16, LANES), F32)
        for t in range(2):
            block = jnp.where(row == t * 4 + k, first[t : t + 1], block)
            if k >= 1:
                block = jnp.where(row == 8 + t * 4 + k - 1, -first[2 + t : 3 + t], block)
            block = jnp.where(row == 8 + t * 4 + k, first[4 + t : 5 + t], block)
        high, low = split(block)
        high32, low32 = high.astype(F32), low.astype(F32)
        tail = jnp.where(
            pad_row == 0,
            bias_high.astype(F32),
            jnp.where(pad_row == 1, bias_low.astype(F32), 0.0),
        )
        tall = jnp.concatenate([high32, high32, low32, tail, jnp.zeros((64, LANES), F32)], 0)
        a1_out[k * HID : (k + 1) * HID, :] = jnp.transpose(tall)[:, :64].astype(BF16)
    second = w2[...]
    for out, matrix in ((w2_out, second), (w2t_out, jnp.transpose(second))):
        high, low = split(matrix)
        out[0:HID, :] = jnp.concatenate([high, high], 1)
        out[HID : 2 * HID, :] = jnp.concatenate([low, low], 1)
    vectors = [b2[...], wh[...]] + [first[f : f + 1] for f in range(6)]
    for n, vector in enumerate(vectors):
        column = jnp.transpose(jnp.broadcast_to(vector, (HID, LANES)))
        col_out[n * HID : (n + 1) * HID, :] = column
    col_out[8 * HID : 8 * HID + 8, :] = jnp.broadcast_to(bh[...], (8, LANES))


def assemble_kernel(
    rows, own_north, near, far, chip, tracer, cot, land, levels, ext, packed
):
    lane = iota((8, LANES), 1)
    lat, n_lat = lax.axis_index("lat"), lax.axis_size("lat")
    at_top = lat == n_lat - 1
    odd = lax.rem(lat, 2) == 1
    at_bottom = lat == 0
    facing = own_north[40 + HALO : 41 + HALO, :].astype(jnp.int32)
    source = jnp.broadcast_to(facing, (8, LANES))
    offset = jnp.broadcast_to(source[:, 0:1], (8, LANES))

    def mirrored(place):
        both = jnp.where(
            lane <= offset, near[place : place + 8, :], far[place : place + 8, :]
        )
        return jnp.take_along_axis(both, source, axis=1)

    zero = jnp.zeros((8, LANES), F32)

    def from_north(place):
        return jnp.where(odd, near[place : place + 8, :], chip[place : place + 8, :])

    def from_south(place):
        below = jnp.where(odd, chip[place : place + 8, :], near[place : place + 8, :])
        return jnp.where(at_bottom, 0.0, below)

    def north(plain, folded):
        return jnp.where(at_top, mirrored(folded), from_north(plain))

    def spread(tile, j):
        return jnp.broadcast_to(tile[j : j + 1], (8, LANES))

    depth_here = (land[...] * levels[...]).astype(F32)
    depth_south = from_south(40)
    depth_north = from_north(40)
    depth_fold = mirrored(40)
    total = rows + 2 * HALO
    tiles = []
    for i in range(total):
        r = i - HALO
        if r < 0:
            tile_c = from_south(8 * i)
            tile_l = from_south(24 + 8 * (i - 1)) if i >= 1 else zero
            tile_n = spread(depth_south, i)
        elif r < rows:
            tile_c = tracer[pl.ds(r, 8, stride=rows), :]
            tile_l = cot[pl.ds(r, 8, stride=rows), :]
            tile_n = spread(depth_here, r)
        else:
            j = r - rows
            tile_c = north(8 * j, 8 * (2 - j))
            tile_l = north(24 + 8 * j, 24 + 8 * (1 - j)) if j < 2 else zero
            tile_n = jnp.where(at_top, spread(depth_fold, 2 - j), spread(depth_north, j))
        tiles.append((tile_c, tile_l, tile_n))
        for part, tile in enumerate(tiles[-1]):
            ext[24 * i + 8 * part : 24 * i + 8 * part + 8, :] = tile
    for part in range(3):
        acc = zero
        for slot in range(rows + 4):
            moved = pltpu.roll(tiles[slot + 1][part], SLOT * slot + HALO, 1)
            inside = (lane >= SLOT * slot) & (lane < SLOT * slot + SLOT)
            acc = jnp.where(inside, moved, acc)
        packed[8 * part : 8 * part + 8, :] = acc


def steps_kernel(
    rows,
    ext,
    east_in,
    west_in,
    a1,
    w2t,
    w2,
    cols,
    out_tracer,
    out_grad,
    out_keep,
    out_give,
    c_tiles0,
    c_tiles1,
    wv_tiles,
    wet_tiles,
    kappa_tiles,
    slope0,
    slope1,
    d3_tiles,
    bar_tiles,
    x0,
    x1,
    h1b0,
    h1b1,
    h1f0,
    h1f1,
    h2f0,
    h2f1,
    acc_w2,
    acc_a1,
    acc_head,
):
    total = rows + 2 * HALO
    lane = iota((8, LANES), 1)
    level = jnp.bitwise_and(iota((8, LANES), 0), DEPTH - 1)
    level_wide = jnp.bitwise_and(iota((8, 2 * LANES), 0), DEPTH - 1)
    zero = jnp.zeros((8, LANES), F32)
    side_tile = rows
    tile_of = {i: i - HALO for i in range(HALO, rows + HALO)}
    place = rows + 1
    for ring in (1, 2, 3):
        tile_of[HALO - ring] = place
        tile_of[rows + HALO - 1 + ring] = place + 1
        place += 2
    n_tiles = place + (place % 2)
    slots = range(1, rows + 5)

    def east(main, side):
        return (
            pltpu.roll(jnp.where(lane == 0, side, main), LANES - 1, 1),
            pltpu.roll(jnp.where(lane == 0, main, side), LANES - 1, 1),
        )

    def from_west(main, side):
        return (
            pltpu.roll(jnp.where(lane == LANES - 1, side, main), 1, 1),
            pltpu.roll(jnp.where(lane == LANES - 1, main, side), 1, 1),
        )

    def from_west_main(main, side):
        return pltpu.roll(jnp.where(lane == LANES - 1, side, main), 1, 1)

    def unpack(tile, i):
        return pltpu.roll(tile, LANES - (SLOT * (i - 1) + HALO), 1)

    def pack(tiles):
        acc = zero
        for i, tile in tiles.items():
            slot = i - 1
            moved = pltpu.roll(tile, SLOT * slot + HALO, 1)
            inside = (lane >= SLOT * slot) & (lane < SLOT * slot + SLOT)
            acc = jnp.where(inside, moved, acc)
        return acc

    def column(n):
        part = cols[n * HID : (n + 1) * HID, :]
        return jnp.concatenate([part, part], 1)

    head_bias = cols[8 * HID : 8 * HID + 1, :][:, 0:1]

    def both(x):
        return x + pltpu.roll(x, 4, 0)

    third = lax.rem(lane, SLOT)
    from_left = third < HALO
    side_c_packed = jnp.where(from_left, west_in[0:8, :], east_in[0:8, :])
    side_l_packed = jnp.where(from_left, west_in[8:16, :], east_in[8:16, :])
    side_n_packed = jnp.where(from_left, west_in[16:24, :], east_in[16:24, :])
    side_lanes = (lane < HALO) | (lane >= LANES - HALO)

    def wet_of(depth):
        return jnp.where(depth > level.astype(F32), 1.0, 0.0)

    def vertical_of(depth):
        inside = (depth > (level + 1).astype(F32)) & (level < DEPTH - 1)
        return jnp.where(inside, 1.0, 0.0)

    def tile_at(i, part):
        place = 24 * i + 8 * part
        return ext[place : place + 8, :]

    c0, wet = {}, {}
    for i in range(total):
        depth = tile_at(i, 2)
        main_c = tile_at(i, 0)
        main_w = wet_of(depth)
        if i in slots:
            side_c = unpack(side_c_packed, i)
            side_w = jnp.where(side_lanes, wet_of(unpack(side_n_packed, i)), 0.0)
        else:
            side_c, side_w = zero, zero
        c0[i] = (main_c, side_c)
        wet[i] = (main_w, side_w)
        c_tiles0[tile_of[i]] = main_c
        wet_tiles[tile_of[i]] = main_w
        wv_tiles[tile_of[i]] = vertical_of(depth)
    c_tiles0[side_tile] = side_c_packed
    wet_tiles[side_tile] = wet_of(side_n_packed)
    wv_tiles[side_tile] = vertical_of(side_n_packed)
    for tile in range(place, n_tiles):
        c_tiles0[tile] = zero
        wet_tiles[tile] = zero
        wv_tiles[tile] = zero

    def closure(start, steps, group, save, c_tiles, slope, xs, h1b, h1f, h2f):
        def body(step, carry):
            first_pair = start + step * group
            items = [(first_pair + g, k) for g in range(group) for k in range(DEPTH)]
            inputs = []
            for g in range(group):
                p = first_pair + g
                pieces = []
                for a in range(2):
                    c = c_tiles[2 * p + a]
                    v = (pltpu.roll(c, 7, 0) - c) * wv_tiles[2 * p + a]
                    pieces.append(jnp.concatenate([c, v], 0))
                high, low = split(jnp.concatenate(pieces, 1))
                x = jnp.concatenate([high, low, high, jnp.ones((16, 2 * LANES), BF16)], 0)
                if save:
                    xs[p] = x
                inputs.append(jnp.dot(a1[...], x, preferred_element_type=F32))
            outs = [jnp.zeros((8, 2 * LANES), F32)] * group
            pairs = {}
            for j in range(len(items) + 1):
                if j < len(items):
                    p, k = items[j]
                    h1 = jnp.tanh(inputs[j // DEPTH][k * HID : (k + 1) * HID])
                    pairs[j] = jnp.concatenate(split(h1), 0)
                    if save:
                        h1f[p, k] = h1
                        h1b[p, k] = pairs[j]
                if j >= 1:
                    p, k = items[j - 1]
                    z = jnp.dot(w2t[...], pairs.pop(j - 1), preferred_element_type=F32)
                    h2 = jnp.tanh(z[:HID] + z[HID:] + column(0))
                    if save:
                        h2f[p, k] = h2
                    head = jnp.sum(h2 * column(1), 0, keepdims=True)
                    g = (j - 1) // DEPTH
                    outs[g] = jnp.where(level_wide == k, head, outs[g])
            for g in range(group):
                sig = jax.nn.sigmoid(outs[g] + head_bias)
                for a in range(2):
                    tile = 2 * (first_pair + g) + a
                    part = sig[:, a * LANES : (a + 1) * LANES]
                    kappa = KMAX * part * wet_tiles[tile]
                    kappa_tiles[tile] = kappa
                    slope[tile] = kappa * (1.0 - part)
            return carry

        if steps == 1:
            body(0, 0)
        else:
            lax.fori_loop(0, steps, body, 0)

    def edge_masks(i):
        east_w = east(*wet[i])
        return tuple(0.5 * a * b for a, b in zip(wet[i], east_w))

    def north_mask(i):
        return tuple(0.5 * a * b for a, b in zip(wet[i], wet[i + 1]))

    def kappas(lo, hi):
        packed = kappa_tiles[side_tile]
        out = {}
        for i in range(lo, hi + 1):
            side = unpack(packed, i) if i in slots else zero
            out[i] = (kappa_tiles[tile_of[i]], side)
        return out

    def coefficients(kappa, lo, hi):
        ce, cn = {}, {}
        for i in range(lo, hi + 1):
            ke = east(*kappa[i])
            ce[i] = tuple(m * (a + b) for m, a, b in zip(edge_masks(i), kappa[i], ke))
        for i in range(lo - 1, hi + 1):
            cn[i] = tuple(
                m * (a + b) for m, a, b in zip(north_mask(i), kappa[i], kappa[i + 1])
            )
        return ce, cn

    def diffs(field, lo, hi):
        de, dn = {}, {}
        for i in range(lo, hi + 1):
            fe = east(*field[i])
            de[i] = tuple(b - a for a, b in zip(field[i], fe))
        for i in range(lo - 1, hi + 1):
            dn[i] = tuple(b - a for a, b in zip(field[i], field[i + 1]))
        return de, dn

    def diffuse(field, ce, cn, de, dn, lo, hi):
        out = {}
        flux_n = {i: tuple(c * d for c, d in zip(cn[i], dn[i])) for i in range(lo - 1, hi + 1)}
        for i in range(lo, hi + 1):
            fe = tuple(c * d for c, d in zip(ce[i], de[i]))
            fw = from_west(*fe)
            out[i] = tuple(
                f + ((a - b) + (c - d))
                for f, a, b, c, d in zip(field[i], fe, fw, flux_n[i], flux_n[i - 1])
            )
        return out

    def kappa_bars(de, dn, le, ln, lo, hi):
        out = {}
        gn = {}
        for i in range(lo - 1, hi + 1):
            gn[i] = tuple(-m * a * b for m, a, b in zip(north_mask(i), dn[i], ln[i]))
        for i in range(lo, hi + 1):
            ge = tuple(-m * a * b for m, a, b in zip(edge_masks(i), de[i], le[i]))
            gw = from_west(*ge)
            out[i] = tuple(
                both((a + b) + (c + d)) for a, b, c, d in zip(ge, gw, gn[i], gn[i - 1])
            )
        return out

    def outer(left, right):
        return lax.dot_general(
            left, right, (((1,), (1,)), ((), ())), preferred_element_type=F32
        )

    sublane_wide = iota((8, 2 * LANES), 0)

    def groups(x):
        return jnp.sum(x.reshape(HID // 8, 8, 2 * LANES), 0)

    def put_row(bars, n, row, part):
        value = jnp.where(sublane_wide == row, jnp.sum(part, 0, keepdims=True), 0.0)
        bars = list(bars)
        bars[n] = plus(bars[n], value)
        return bars

    def plus(left, right):
        return right if left is None else left + right

    def closure_back(start, steps, group, with_sums, slope, xs, h1b, h1f, h2f):
        def body(step, carry):
            first_pair = start + step * group
            items = [(first_pair + g, k) for g in range(group) for k in range(DEPTH)]
            d3 = [
                jnp.concatenate(
                    [
                        d3_tiles[2 * (first_pair + g) + a] * slope[2 * (first_pair + g) + a]
                        for a in range(2)
                    ],
                    1,
                )
                for g in range(group)
            ]
            bars = [[None] * 6 for g in range(group)]
            sum_w2, sum_head, sum_a1 = None, None, None
            seconds, firsts = {}, {}
            for j in range(len(items) + 2):
                if j < len(items):
                    p, k = items[j]
                    h2 = h2f[p, k]
                    row = d3[j // DEPTH][k : k + 1]
                    d2 = (column(1) * row) * (1.0 - h2 * h2)
                    seconds[j] = jnp.concatenate(split(d2), 0)
                    if with_sums:
                        sum_head = plus(sum_head, h2 * row)
                if 1 <= j <= len(items):
                    p, k = items[j - 1]
                    d2b = seconds.pop(j - 1)
                    e = jnp.dot(w2[...], d2b, preferred_element_type=F32)
                    h1 = h1f[p, k]
                    d1 = (e[:HID] + e[HID:]) * (1.0 - h1 * h1)
                    firsts[j - 1] = d1
                    if with_sums:
                        sum_w2 = plus(sum_w2, outer(h1b[p, k], d2b))
                if j >= 2:
                    p, k = items[j - 2]
                    g = (j - 2) // DEPTH
                    d1 = firsts.pop(j - 2)
                    if with_sums:
                        seconds[g, k] = jnp.concatenate(split(d1), 0)
                        if k == DEPTH - 1:
                            d1b = jnp.concatenate([seconds.pop((g, n)) for n in range(DEPTH)], 0)
                            sum_a1 = plus(sum_a1, outer(d1b, xs[p, 0:32, :]))
                    parts = [groups(d1 * column(2 + f)) for f in range(6)]
                    for t in range(2):
                        bars[g] = put_row(bars[g], t, t * DEPTH + k, parts[t])
                        if k >= 1:
                            below = bars[g][2 + t]
                            bars[g] = put_row(
                                bars[g], 4 + t, t * DEPTH + k - 1, below - parts[2 + t]
                            )
                        bars[g][2 + t] = parts[4 + t]
            if with_sums:
                acc_w2[...] += sum_w2
                acc_head[...] += sum_head
                acc_a1[...] += sum_a1
            for g in range(group):
                cells = plus(bars[g][0], bars[g][1])
                vertical = plus(bars[g][4], bars[g][5])
                for a in range(2):
                    tile = 2 * (first_pair + g) + a
                    lanes = slice(a * LANES, (a + 1) * LANES)
                    v = vertical[:, lanes] * wv_tiles[tile]
                    bar_tiles[tile] = cells[:, lanes] - v + pltpu.roll(v, 1, 0)
            return carry

        if steps == 1:
            body(0, 0)
        else:
            lax.fori_loop(0, steps, body, 0)

    low, high = HALO, rows + HALO - 1
    step0 = (c_tiles0, slope0, x0, h1b0, h1f0, h2f0)
    own = rows // 2
    closure(0, own // GROUP, GROUP, True, *step0)
    closure(own, 1, n_tiles // 2 - own, False, *step0)
    kappa0 = kappas(0, total - 1)
    ce0, cn0 = coefficients(kappa0, low - 2, high + 2)
    de0, dn0 = diffs(c0, low - 2, high + 2)
    c1 = diffuse(c0, ce0, cn0, de0, dn0, low - 2, high + 2)
    for i in range(low - 2, high + 3):
        c_tiles1[tile_of[i]] = c1[i][0]
    c_tiles1[side_tile] = pack({i: c1[i][1] for i in range(low - 2, high + 3)})
    tiles1 = rows + 5
    for tile in range(tiles1, n_tiles):
        c_tiles1[tile] = zero
    step1 = (c_tiles1, slope1, x1, h1b1, h1f1, h2f1)
    closure(0, own // GROUP, GROUP, True, *step1)
    closure(own, 1, 2, True, *step1)
    closure(own + 2, 1, 1, False, *step1)
    kappa1 = kappas(low - 2, high + 2)
    ce1, cn1 = coefficients(kappa1, low - 1, high + 1)
    de1, dn1 = diffs(c1, low - 1, high + 1)
    c2 = diffuse(c1, ce1, cn1, de1, dn1, low, high)
    for i in range(low, high + 1):
        out_tracer[pl.ds(i - low, 8, stride=rows), :] = c2[i][0]
    lam2 = {}
    for i in range(low - 2, high + 3):
        lam2[i] = (tile_at(i, 1), unpack(side_l_packed, i))
    le, ln = diffs(lam2, low - 1, high + 1)
    direct = diffuse(lam2, ce1, cn1, le, ln, low - 1, high + 1)
    bars = kappa_bars(de1, dn1, le, ln, low - 1, high + 1)
    for i in range(low - 1, high + 2):
        d3_tiles[tile_of[i]] = bars[i][0]
    d3_tiles[side_tile] = pack({i: bars[i][1] for i in range(low, high + 1)})
    d3_tiles[rows + 3] = zero
    acc_w2[...] = jnp.zeros_like(acc_w2)
    acc_a1[...] = jnp.zeros_like(acc_a1)
    acc_head[...] = jnp.zeros_like(acc_head)
    closure_back(0, own // GROUP, GROUP, True, *step1[1:])
    closure_back(own, 1, 2, False, *step1[1:])
    side_bar = bar_tiles[side_tile]
    lam1 = {}
    for i in range(low - 1, high + 2):
        main = direct[i][0] + bar_tiles[tile_of[i]]
        side = direct[i][1] + unpack(side_bar, i)
        lam1[i] = (main, side)
    le, ln = diffs(lam1, low, high)
    direct = diffuse(lam1, ce0, cn0, le, ln, low, high)
    bars = kappa_bars(de0, dn0, le, ln, low, high)
    for i in range(low, high + 1):
        d3_tiles[tile_of[i]] = bars[i][0]
    closure_back(0, own // GROUP, GROUP, True, *step0[1:])
    for i in range(low, high + 1):
        out_grad[pl.ds(i - low, 8, stride=rows), :] = direct[i][0] + bar_tiles[tile_of[i]]
    first = [None] * 6

    def add(f, value):
        first[f] = value if first[f] is None else first[f] + value

    for k in range(DEPTH):
        cells = acc_a1[2 * HID * k : 2 * HID * k + HID, :]
        cells = cells + acc_a1[2 * HID * k + HID : 2 * HID * (k + 1), :]
        cells = jnp.concatenate([cells, jnp.zeros((HID, LANES - 32), F32)], 1)
        turned = jnp.transpose(cells)
        turned = turned[0:16] + turned[16:32]
        for t in range(2):
            add(t, turned[t * 4 + k : t * 4 + k + 1])
            if k >= 1:
                add(2 + t, -turned[8 + t * 4 + k - 1 : 8 + t * 4 + k])
            add(4 + t, turned[8 + t * 4 + k : 8 + t * 4 + k + 1])
    head = jnp.sum(jnp.transpose(acc_head[:, :LANES] + acc_head[:, LANES:]), 0, keepdims=True)
    rest = jnp.concatenate(first + [head, jnp.zeros_like(head)], 0)
    second = (acc_w2[:HID, :HID] + acc_w2[HID:, HID:]) + (acc_w2[:HID, HID:] + acc_w2[HID:, :HID])
    odd = jnp.bitwise_and(lax.axis_index("lat"), 1) == 1
    left, right = second[: HID // 2], second[HID // 2 :]
    out_keep[0 : HID // 2, :] = jnp.where(odd, right, left)
    out_give[0 : HID // 2, :] = jnp.where(odd, left, right)
    out_keep[HID // 2 :, :] = jnp.where(odd, 0.0, rest)
    out_give[HID // 2 :, :] = jnp.where(odd, rest, 0.0)


def finish_kernel(scale, mine, other, w1_out, w2_out, wh_out):
    odd = jnp.bitwise_and(lax.axis_index("lat"), 1) == 1
    half = HID // 2
    a, b = mine[...], other[...]
    left, right = jnp.where(odd, b, a) * scale, jnp.where(odd, a, b) * scale
    w2_out[0:half, :] = left[:half]
    w2_out[half:, :] = right[:half]
    w1_out[...] = left[half : half + 6]
    wh_out[...] = left[half + 6 : half + 7]


VMEM = pl.BlockSpec(memory_space=pltpu.VMEM)
SMEM = pl.BlockSpec(memory_space=pltpu.SMEM)
HBM = pl.BlockSpec(memory_space=pltpu.HBM)


def call(kernel, outs, ins, out_specs=None, scratch=(), limit=4 * 1024 * 1024, flops=1_000_000, size=1_000_000):
    return pl.pallas_call(
        kernel,
        out_shape=outs,
        in_specs=ins,
        out_specs=out_specs or [VMEM] * len(outs),
        scratch_shapes=list(scratch),
        compiler_params=pltpu.CompilerParams(vmem_limit_bytes=limit),
        cost_estimate=pl.CostEstimate(flops=flops, bytes_accessed=size, transcendentals=0),
    )


def shape(*dims, dtype=F32):
    return jax.ShapeDtypeStruct(dims, dtype)


def per_device(
    tracers,
    land_mask,
    level_counts,
    fold_partner,
    cotangent,
    w_first,
    b_first,
    w_second,
    b_second,
    w_head,
    b_head,
):
    rows, cols = land_mask.shape
    n_lon, n_lat = lax.axis_size("lon"), lax.axis_size("lat")
    tracer2 = tracers.reshape(8 * rows, cols)
    cot2 = cotangent.reshape(8 * rows, cols)

    args = (tracer2, cot2, land_mask, level_counts, fold_partner)
    near_rows, north_rows, chip_rows, turn = call(
        functools.partial(edges_kernel, rows, cols),
        [shape(48, LANES)] * 3 + [shape(1, dtype=jnp.int32)],
        [HBM] * len(args),
        out_specs=[VMEM] * 3 + [SMEM],
        scratch=[pltpu.VMEM(x.shape, x.dtype) for x in args[:4]]
        + [pltpu.SMEM(fold_partner.shape, fold_partner.dtype)]
        + [pltpu.SemaphoreType.DMA((len(args),))],
        limit=None,
    )(*args)

    def exchange(j, near, far, chip):
        top = n_lat - 1

        def send(x, plain, fold):
            pairs = [
                (b * n_lat + source, b * n_lat + target)
                for b in range(n_lon)
                for source, target in plain
            ]
            if fold is not None:
                pairs += [
                    (b * n_lat + top, ((fold - b) % n_lon) * n_lat + top) for b in range(n_lon)
                ]
            return lax.ppermute(x, ("lon", "lat"), pairs)

        middle = [(0, 0)] + [(i, ((i + 1) ^ 1) - 1) for i in range(1, top)]
        return (
            send(near, middle, j),
            send(far, [(i, i) for i in range(top)], j - 1),
            send(chip, [(i, i ^ 1) for i in range(n_lat)], None),
        )

    near, far, chip = lax.switch(
        turn[0],
        [functools.partial(exchange, j) for j in range(n_lon)],
        near_rows,
        north_rows,
        chip_rows,
    )

    total = rows + 2 * HALO
    ext, packed = call(
        functools.partial(assemble_kernel, rows),
        [shape(24 * total, LANES), shape(24, LANES)],
        [VMEM] * 8,
    )(
        north_rows,
        near,
        far,
        chip,
        tracer2,
        cot2,
        land_mask,
        level_counts,
    )
    a1, w2t, w2, cols_w = call(
        weights_kernel,
        [
            shape(DEPTH * HID, 64, dtype=BF16),
            shape(2 * HID, 2 * HID, dtype=BF16),
            shape(2 * HID, 2 * HID, dtype=BF16),
            shape(8 * HID + 8, LANES),
        ],
        [VMEM] * 6,
    )(
        w_first,
        b_first.reshape(1, HID),
        w_second,
        b_second.reshape(1, HID),
        w_head.reshape(1, HID),
        b_head.reshape(1, 1),
    )
    from_east = lax.ppermute(packed, "lon", [((i + 1) % n_lon, i) for i in range(n_lon)])
    from_west = lax.ppermute(packed, "lon", [(i, (i + 1) % n_lon) for i in range(n_lon)])

    n_tiles = total + 1 + (total + 1) % 2
    pairs0 = rows // 2
    pairs1 = rows // 2 + 2
    tiles = pltpu.VMEM((n_tiles, 8, LANES), F32)
    wide = 2 * LANES
    scratch = (
        [tiles] * 9
        + [pltpu.VMEM((n, 64, wide), BF16) for n in (pairs0, pairs1)]
        + [pltpu.VMEM((n, DEPTH, 2 * HID, wide), BF16) for n in (pairs0, pairs1)]
        + [pltpu.VMEM((n, DEPTH, HID, wide), F32) for n in (pairs0, pairs1)]
        + [pltpu.VMEM((n, DEPTH, HID, wide), F32) for n in (pairs0, pairs1)]
        + [
            pltpu.VMEM((2 * HID, 2 * HID), F32),
            pltpu.VMEM((DEPTH * 2 * HID, 32), F32),
            pltpu.VMEM((HID, wide), F32),
        ]
    )
    final, grad, keep, give = call(
        functools.partial(steps_kernel, rows),
        [shape(8 * rows, LANES)] * 2 + [shape(HID // 2 + 8, LANES)] * 2,
        [VMEM] * 7,
        scratch=scratch,
        limit=36 * 1024 * 1024,
        flops=10_000_000_000,
    )(ext, from_east, from_west, a1, w2t, w2, cols_w)

    def swap(x, mask):
        pairs = [(i, i ^ mask) for i in range(n_lon * n_lat)]
        return lax.ppermute(x, ("lon", "lat"), pairs)

    sums = keep + swap(give, 1)
    bits = [1 << b for b in range(1, (n_lon * n_lat).bit_length() - 1)]
    while bits:
        a, bits = bits[0], bits[1:]
        if bits:
            b, bits = bits[0], bits[1:]
            near, far, both = swap(sums, a), swap(sums, b), swap(sums, a | b)
            sums = (sums + near) + (far + both)
        else:
            sums = sums + swap(sums, a)
    other = swap(sums, 1)
    scale = 1.0 / math.sqrt(n_lon * cols * n_lat * rows * DEPTH)
    first_grad, second_grad, head_grad = call(
        functools.partial(finish_kernel, scale),
        [shape(6, HID), shape(HID, HID), shape(1, HID)],
        [VMEM] * 2,
    )(sums, other)
    return (
        final.reshape(tracers.shape),
        grad.reshape(tracers.shape),
        first_grad,
        second_grad,
        head_grad.reshape(HID),
    )


def solution(mesh):
    return jax.shard_map(
        per_device,
        mesh=mesh,
        in_specs=(
            P(None, None, "lat", "lon"),
            P("lat", "lon"),
            P("lat", "lon"),
            P("lon"),
            P(None, None, "lat", "lon"),
            P(),
            P(),
            P(),
            P(),
            P(),
            P(),
        ),
        out_specs=(P(None, None, "lat", "lon"), P(None, None, "lat", "lon"), P(), P(), P()),
        check_vma=False,
    )
```
